256 devices in a mesh: gz: 32 (over z, y_lo, core), mat: 8 (over x, y_hi).
Axes of the slice: x: 4, y: 4 (y_hi: 2, y_lo: 2; y = y_hi * 2 + y_lo), z: 8, core: 2. Of those that a mesh axis runs over, the one named last changes fastest.
Arguments:
- particle_mass: float32 [8, 4194304], P('mat', 'gz'), may hold values from 0.5 to 2
- particle_velocity: float32 [8, 3, 4194304], P('mat', None, 'gz'), may hold values from -6 to 6
- spline_weights: float32 [8, 9, 4194304], P('mat', None, 'gz'), as said below
- particle_cells: int32 [8, 4194304], P('mat', 'gz'), may hold values from 0 to 2047, as said below
- block_counts: int32 [8, 32, 32], P('mat', 'gz'), may hold values from 512 to 4096, as said below
- friction: float32 [8], P('mat'), may hold values from 0.1 to 0.8
- contact_flags: int32 [64, 256, 128], P('gz'), may hold values 0 or 1
Outputs:
- grid_velocity: float32 [8, 3, 64, 256, 128], P('mat', None, 'gz')
The draws below stay inside these ranges and needn't reach their ends.
Inputs may be any that keep to these rules, and one draw needn't show every extreme that they name: `spline_weights`: rows 3 a, 3 a + 1, 3 a + 2 hold the quadratic B-spline weights along axis a (z, x, y) for the nodes at offsets -1, 0, +1 from the particle's cell; each triple sums to 1. `particle_cells`: each value is (z * 8 + u) * 128 + y with z < 2 and u < 8, the cell inside the particle's block; the slots of a block are in nondecreasing Morton order of that cell. `block_counts`: the live slots of a block are its first ones; the rest are padding.
All inputs are finite; a program needn't handle non-finite values. No bound on the sum of `contact_flags` on one device may be relied on, other than what follows from the above.
Results may differ from the reference program's by a relative error of at most 0.007.
Values may be sent and summed in bfloat16 or wider, within the bound.
A program may use at most 64 MiB of HBM per device.

```python
import math
import jax
import jax.numpy as jnp
from jax import lax

CZ = 2
GX = 256
GY = 128
BW = 8
XB = 32
SLOTS = 4096
CAP = 131072
SLABS = 32
PTOT = 4194304
NZ = 64
MATS = 8


def draw_spline_weights(key, part):
    key = jax.random.fold_in(key, 11)
    uniform_values = jax.random.uniform(key, (MATS, 3, PTOT), jnp.float32)
    offset = uniform_values
    first_tap = 0.5 * (1.0 - offset) * (1.0 - offset)
    middle_tap = 0.75 - (offset - 0.5) * (offset - 0.5)
    last_tap = 0.5 * offset * offset
    return jnp.stack([first_tap, middle_tap, last_tap], axis=2).reshape(MATS, 9, PTOT)


def draw_particle_cells(key, part):
    key = jax.random.fold_in(key, 23)
    row_count = MATS * SLABS * XB
    key_z, key_x, key_y = jax.random.split(key, 3)
    layers_z = jax.random.randint(key_z, (row_count, SLOTS), 0, CZ)
    column = jax.random.randint(key_x, (row_count, SLOTS), 0, BW)
    row_y = jax.random.randint(key_y, (row_count, SLOTS), 0, GY)
    morton_code = jnp.zeros((row_count, SLOTS), jnp.int32)
    for bit_level in range(3):
        morton_code = morton_code + ((layers_z >> bit_level & 1) << 3 * bit_level + 2)
        morton_code = morton_code + ((column >> bit_level & 1) << 3 * bit_level + 1)
        morton_code = morton_code + ((row_y >> bit_level & 1) << 3 * bit_level)
    morton_code = morton_code + ((row_y >> 3) * 64 + (layers_z >> 3) << 9)
    sort_order = jnp.argsort(morton_code, axis=1, stable=True)
    layers_z = jnp.take_along_axis(layers_z, sort_order, axis=1)
    column = jnp.take_along_axis(column, sort_order, axis=1)
    row_y = jnp.take_along_axis(row_y, sort_order, axis=1)
    cell_index = (layers_z * BW + column) * GY + row_y
    return cell_index.reshape(MATS, PTOT).astype(jnp.int32)


def draw_block_counts(key, part):
    key = jax.random.fold_in(key, 37)
    key_level, key_base, key_top, key_low = jax.random.split(key, 4)
    entries = SLABS * XB
    levels = jax.random.randint(key_level, (MATS, SLABS, 1), 1, 9)
    base_draw = jax.random.randint(key_base, (MATS, SLABS, XB), 0, SLOTS + 1)
    counts = jnp.minimum(SLOTS // 8 + levels * base_draw // 8, SLOTS)
    flat_counts = counts.reshape(MATS, entries)
    top_place = jax.random.randint(key_top, (MATS, 1), 0, entries)
    low_place = (top_place + 1 + jax.random.randint(key_low, (MATS, 1), 0, entries - 1)) % entries
    positions = jnp.arange(entries, dtype=jnp.int32)[None, :]
    flat_counts = jnp.where(positions == top_place, SLOTS, flat_counts)
    flat_counts = jnp.where(positions == low_place, SLOTS // 8, flat_counts)
    return flat_counts.reshape(MATS, SLABS, XB).astype(jnp.int32)


def touch_ends(values, own_key, least, largest):
    place = [jax.random.randint(jax.random.fold_in(own_key, axis), (), 0, length) for axis, length in enumerate(values.shape)]
    widest = values.shape.index(max(values.shape))
    next_to = place[:widest] + [(place[widest] + 1) % values.shape[widest]] + place[widest + 1:]
    return values.at[tuple(place)].set(least).at[tuple(next_to)].set(largest)


def block_levels(key, extent, shards, low, largest):
    level, own = 1.0, jax.random.fold_in(key, 6)
    for dim, shards_of in shards:
        draws = jnp.exp(jax.random.uniform(jax.random.fold_in(own, dim), (shards_of,), jnp.float32, low / len(shards), largest / len(shards)))
        level = level * jnp.repeat(draws, extent[dim] // shards_of).reshape([-1 if axis == dim else 1 for axis in range(len(extent))])
    return level


def scatter_about(rng, extent, width, most, pieces=(), kind=jnp.bfloat16):
    loudness = block_levels(rng, extent, pieces, -0.22, 0.18) if pieces else 1.0
    drawn = jax.random.normal(rng, extent, jnp.float32) * width * loudness
    return jnp.minimum(jnp.maximum(drawn, -most), most).astype(kind)


def setup_inputs(seed: int = 0) -> dict:
    seeds = jax.random.split(jax.random.key(seed), 8)
    particle_mass = jnp.clip(jnp.exp(math.log(2.0) - 1.3862944 * jax.random.uniform(seeds[0], (MATS, PTOT), jnp.float32) ** block_levels(seeds[0], (MATS, PTOT), ((0, 8), (1, 32)), -0.2, 0.2)), 0.5, 2.0)
    particle_velocity = scatter_about(seeds[1], (MATS, 3, PTOT), 1.0, 6.0, ((0, 8), (2, 32)), jnp.float32)
    spline_weights = draw_spline_weights(jax.random.fold_in(seeds[7], 71), 0)
    particle_cells = draw_particle_cells(jax.random.fold_in(seeds[7], 71), 0)
    block_counts = draw_block_counts(jax.random.fold_in(seeds[7], 71), 0)
    friction = jnp.clip(jnp.exp(math.log(0.8) - 2.0794415 * jax.random.uniform(seeds[5], (MATS,), jnp.float32) ** block_levels(seeds[5], (MATS,), ((0, 8),), -0.2, 0.2)), 0.1, 0.8)
    contact_flags = touch_ends((jax.random.randint(seeds[6], (NZ, GX, GY), 0, 2) < 1).astype(jnp.int32), jax.random.fold_in(seeds[6], 1), 0, 1)
    return {"particle_mass": particle_mass, "particle_velocity": particle_velocity, "spline_weights": spline_weights, "particle_cells": particle_cells, "block_counts": block_counts, "friction": friction, "contact_flags": contact_flags}


MASS_FLOOR = 0.2
GRADIENT_FLOOR = 0.1
SLIP_FLOOR = 0.05

def to_half(values):
    return lax.optimization_barrier(values.astype(jnp.bfloat16)).astype(jnp.float32)

def deposit_material(operands):
    masses, velocity, weights, cell_ids, counts = operands
    particle_ids = jnp.arange(PTOT, dtype=jnp.int32)
    slab_of = particle_ids // CAP
    block_of = particle_ids // SLOTS % XB
    slot_of = particle_ids % SLOTS
    live_slots = (slot_of < counts[slab_of, block_of]).astype(jnp.float32)
    carried = jnp.stack([masses, masses * velocity[0], masses * velocity[1], masses * velocity[2]]) * live_slots
    layer_z = cell_ids // (BW * GY)
    column = block_of * BW + cell_ids // GY % BW
    row_y = cell_ids % GY
    global_z = slab_of * CZ + layer_z
    segments = (NZ + 2) * GX * GY
    totals = jnp.zeros((segments, 4), jnp.float32)
    for z_tap in range(3):
        lifted = carried * weights[z_tap]
        for x_tap in range(3):
            left_part = to_half(lifted * weights[3 + x_tap])
            node_x = (column + x_tap - 1) % GX
            for y_tap in range(3):
                node_y = (row_y + y_tap - 1) % GY
                target = ((global_z + z_tap) * GX + node_x) * GY + node_y
                contribution = left_part * to_half(weights[6 + y_tap])
                totals = totals + jax.ops.segment_sum(contribution.T, target.astype(jnp.int32), num_segments=segments)
    grid_nodes = totals.T.reshape(4, NZ + 2, GX, GY)
    return grid_nodes[:, 1:NZ + 1]

def correct_nodes(node_fields, extended, center, friction_value, flag_values):
    node_mass = extended[1:-1]
    grad_z = (extended[2:] - extended[:-2]) * 0.5
    grad_x = (jnp.roll(node_mass, -1, axis=1) - jnp.roll(node_mass, 1, axis=1)) * 0.5
    grad_y = (jnp.roll(node_mass, -1, axis=2) - jnp.roll(node_mass, 1, axis=2)) * 0.5
    length = jnp.sqrt(grad_z * grad_z + grad_x * grad_x + grad_y * grad_y)
    normal = jnp.stack([grad_z, grad_x, grad_y]) / jnp.maximum(length, GRADIENT_FLOOR)
    node_speed = node_fields[1:] / jnp.maximum(node_fields[0], MASS_FLOOR)
    relative = node_speed - center
    normal_part = relative[0] * normal[0] + relative[1] * normal[1] + relative[2] * normal[2]
    approach = jnp.maximum(normal_part, 0.0)
    tangent = relative - normal_part * normal
    slip_speed = jnp.sqrt(tangent[0] * tangent[0] + tangent[1] * tangent[1] + tangent[2] * tangent[2])
    factor = jnp.minimum(friction_value * approach, slip_speed) / jnp.maximum(slip_speed, SLIP_FLOOR)
    return node_speed - flag_values * (approach * normal + factor * tangent)

def reference(particle_mass, particle_velocity, spline_weights, particle_cells, block_counts, friction, contact_flags):
    all_nodes = lax.map(deposit_material, (particle_mass, particle_velocity, spline_weights, particle_cells, block_counts))
    summed = lax.optimization_barrier(jnp.sum(to_half(all_nodes), axis=0))
    center = summed[1:] / jnp.maximum(summed[0], MASS_FLOOR)
    flag_values = contact_flags.astype(jnp.float32)

    def finish(operands):
        node_fields, friction_value = operands
        extended = jnp.pad(node_fields[0], ((1, 1), (0, 0), (0, 0)))
        return correct_nodes(node_fields, extended, center, friction_value, flag_values)
    return lax.map(finish, (all_nodes, friction))
```

```python
import functools
import jax, jax.numpy as jnp
from jax import lax
from jax.sharding import PartitionSpec as P
from jax.experimental import pallas as pl
from jax.experimental.pallas import tpu as pltpu

BLOCKS=32; SLOTS=4096; W=32
BPS=4
ROWS=SLOTS//128
F32=jnp.float32; BF=jnp.bfloat16

def rows_const(n, fn, k):
    r = lax.broadcasted_iota(jnp.int32, (n, k), 0)
    return fn(r).astype(F32).astype(BF)

def dep_kernel(cfg, counts, mass, vel, wt, cells, out, acc):
    variant, skip, pre = cfg
    step = pl.program_id(0)
    ycon = [rows_const(W, lambda r, t=t: r - t, 128) for t in range(3)]
    xcon = [rows_const(16, lambda r, p=p: (r - p + 1) & 15, 128) for p in range(3)]
    zero = jnp.zeros((), BF)
    sub = lax.broadcasted_iota(jnp.int32, (8, 128), 0)
    place_id = sub * 128 + lax.broadcasted_iota(jnp.int32, (8, 128), 1)
    odd = (sub & 1) == 1

    @pl.when(step == 0)
    def _():
        out[...] = jnp.zeros_like(out)

    def bc(tile, r, rows):
        return jnp.broadcast_to(tile[r:r+1], (rows, 128)).astype(BF)

    def block(i, _):
        b = step * BPS + i
        n = counts[b]
        acc[...] = jnp.zeros_like(acc)
        def sl(g):
            return pl.ds(pl.multiple_of(i * ROWS + g * 8, 8), 8)
        def scan(g):
            y = cells[sl(g), :] & 127
            first = jnp.broadcast_to(y[:, 0:1], (8, 128)) & ~7
            first = jnp.where(odd, pltpu.roll(first, 1, 0), first)
            yrel = y - first
            live = place_id < n - g * 1024
            more = jnp.max(jnp.where(live, yrel, 0)) >= 24
            return [first[2*j, 0] for j in range(4)], more, yrel.astype(F32)
        def prep(g):
            cl = cells[sl(g), :]
            m = jnp.where(place_id < n - g * 1024, mass[sl(g), :], 0.0)
            u = ((cl >> 7) & 7).astype(F32)
            top = cl >= 1024
            car = [m] + [m * vel[k, sl(g), :] for k in range(3)]
            w = [wt[r, sl(g), :] for r in range(9)]
            zn = [jnp.where(top, 0.0, w[0]), jnp.where(top, w[0], w[1]),
                  jnp.where(top, w[1], w[2]), jnp.where(top, w[2], 0.0)]
            return u, car, w, zn
        def xwin(u, w, r):
            ub = bc(u, r, 16)
            xw = jnp.where(ub == xcon[0], bc(w[3], r, 16), zero)
            xw = jnp.where(ub == xcon[1], bc(w[4], r, 16), xw)
            return jnp.where(ub == xcon[2], bc(w[5], r, 16), xw)
        def ywin(yrel, w, r):
            yb = bc(yrel, r, W)
            yw = jnp.where(yb == ycon[0], bc(w[6], r, W), zero)
            yw = jnp.where(yb == ycon[1], bc(w[7], r, W), yw)
            return jnp.where(yb == ycon[2], bc(w[8], r, W), yw)
        def sides(yrel, u, car, w, zn, r):
            xw = xwin(u, w, r)
            yw = ywin(yrel, w, r)
            if variant == 0:
                left = jnp.concatenate([bc(car[f] * zn[z], r, 16) * xw for f in range(4) for z in range(4)], 0)
                return left, yw
            left = jnp.concatenate([bc(zn[z], r, 16) * xw for z in range(4)], 0)
            right = jnp.concatenate([bc(car[f], r, W) * yw for f in range(4)], 0)
            return left, right
        def product(yrel, data, j):
            l0, r0 = sides(yrel, *data, 2 * j)
            l1, r1 = sides(yrel, *data, 2 * j + 1)
            left = jnp.concatenate([l0, l1], 1)
            right = jnp.concatenate([r0, r1], 1)
            return lax.dot_general(right, left, (((1,), (1,)), ((), ())), preferred_element_type=F32)
        def add(base, res):
            rows = pl.ds(pl.multiple_of(base, 8), W)
            if variant == 0:
                acc[rows, :] += res
            else:
                for f in range(4):
                    acc[f, rows, 0:64] += res[f * W:(f + 1) * W]
        def group(g, carry):
            bases, more, yrel = scan(g) if not pre else carry
            data = prep(g)
            nxt = scan(jnp.minimum(g + 1, ROWS // 8 - 1)) if pre else 0
            res = [product(yrel, data, j) for j in range(4)]
            for j in range(4):
                add(bases[j], res[j])
            @pl.when(more)
            def _():
                def window(off, _):
                    shift = (off * W).astype(F32)
                    for j in range(4):
                        base = bases[j] + off * W
                        @pl.when(base < 130)
                        def _():
                            add(base, product(yrel - shift, data, j))
                    return 0
                lax.fori_loop(1, 5, window, 0)
            return nxt
        if skip != 1:
            lax.fori_loop(0, (n + 1023) // 1024, group, scan(0) if pre else 0)
        up = lax.rem(b + 1, BLOCKS); dn = lax.rem(b + BLOCKS - 1, BLOCKS)
        def place(f, z, own, halo):
            out[f, z, pl.ds(pl.multiple_of(b * 8, 8), 8), :] += own
            out[f, z, pl.ds(pl.multiple_of(up * 8, 8), 8), :] += jnp.where(sub == 0, halo, 0.0)
            out[f, z, pl.ds(pl.multiple_of(dn * 8, 8), 8), :] += jnp.where(sub == 7, halo, 0.0)
        if skip == 2:
            return 0
        if variant == 0:
            acc[128:129] += acc[0:1]
            acc[1:2] += acc[129:130]
            t = acc[1:129, :].T
            for f in range(4):
                for z in range(4):
                    o = (f * 4 + z) * 16
                    place(f, z, t[o:o+8], t[o+8:o+16])
        else:
            for f in range(4):
                acc[f, 128:129] += acc[f, 0:1]
                acc[f, 1:2] += acc[f, 129:130]
                t = acc[f, 1:129, :].T
                for z in range(4):
                    o = z * 16
                    place(f, z, t[o:o+8], t[o+8:o+16])
        return 0
    lax.fori_loop(0, BPS, block, 0)

def deposit(cfg, counts, mass, vel, wt, cells):
    variant = cfg[0]
    R = BPS * ROWS
    accs = pltpu.VMEM((160, 256), F32) if variant == 0 else pltpu.VMEM((4, 160, 128), F32)
    return pl.pallas_call(
        functools.partial(dep_kernel, cfg),
        grid=(BLOCKS // BPS,),
        in_specs=[pl.BlockSpec(memory_space=pltpu.SMEM),
                  pl.BlockSpec((R, 128), lambda i: (i, 0)),
                  pl.BlockSpec((3, R, 128), lambda i: (0, i, 0)),
                  pl.BlockSpec((9, R, 128), lambda i: (0, i, 0)),
                  pl.BlockSpec((R, 128), lambda i: (i, 0))],
        out_specs=pl.BlockSpec((4, 4, 256, 128), lambda i: (0, 0, 0, 0)),
        out_shape=jax.ShapeDtypeStruct((4, 4, 256, 128), F32),
        scratch_shapes=[accs],
        compiler_params=pltpu.CompilerParams(vmem_limit_bytes=50 << 20),
    )(counts, mass.reshape(1024, 128), vel.reshape(3, 1024, 128), wt.reshape(9, 1024, 128), cells.reshape(1024, 128))

MASS_FLOOR = 0.2
GRADIENT_FLOOR = 0.1
SLIP_FLOOR = 0.05
PIECES = 8
COLS = 32
MESH = pl.DeviceIdType.MESH


def comm_kernel(fric, dep, flags, out, hsend, hrecv, nf, mass, gradz, rsend, rrecv, cbuf,
                h_ss, h_rs, r_ss, r_rs, c_ss, c_rs):
    slabs = lax.axis_size("gz")
    g = lax.axis_index("gz")
    me = lax.axis_index("mat")
    lo = lax.rem(g + slabs - 1, slabs)
    hi = lax.rem(g + 1, slabs)
    s_lo = jnp.where(g == 0, 0.0, 1.0)
    s_hi = jnp.where(g == slabs - 1, 0.0, 1.0)

    barrier = pltpu.get_barrier_semaphore()
    for other in (lo, hi):
        pl.semaphore_signal(barrier, inc=1, device_id={"gz": other, "mat": me}, device_id_type=MESH)
    for k in range(1, PIECES):
        pl.semaphore_signal(barrier, inc=1, device_id={"gz": g, "mat": lax.rem(me + k, PIECES)},
                            device_id_type=MESH)

    def halo(side, p):
        return pltpu.make_async_remote_copy(
            src_ref=hsend.at[side, p], dst_ref=hrecv.at[side, p],
            send_sem=h_ss.at[side, p], recv_sem=h_rs.at[side, p],
            device_id={"gz": lo if side == 0 else hi, "mat": me}, device_id_type=MESH)

    def share(p):
        return pltpu.make_async_remote_copy(
            src_ref=rsend.at[p], dst_ref=rrecv.at[me], send_sem=r_ss.at[p], recv_sem=r_rs.at[me],
            device_id={"gz": g, "mat": p}, device_id_type=MESH)

    def shared(p):
        return pltpu.make_async_remote_copy(
            src_ref=rsend.at[p], dst_ref=rrecv.at[p], send_sem=r_ss.at[p], recv_sem=r_rs.at[p],
            device_id={"gz": g, "mat": p}, device_id_type=MESH)

    def spread(p):
        return pltpu.make_async_remote_copy(
            src_ref=cbuf.at[me], dst_ref=cbuf.at[me], send_sem=c_ss.at[p], recv_sem=c_rs.at[me],
            device_id={"gz": g, "mat": p}, device_id_type=MESH)

    def spreaded(p):
        return pltpu.make_async_remote_copy(
            src_ref=cbuf.at[p], dst_ref=cbuf.at[p], send_sem=c_ss.at[p], recv_sem=c_rs.at[p],
            device_id={"gz": g, "mat": p}, device_id_type=MESH)

    def cols(p):
        return pl.ds(pl.multiple_of(p * COLS, COLS), COLS)

    def pack(k, _):
        p = lax.rem(me + 1 + k, PIECES)
        x = cols(p)
        for f in range(4):
            hsend[0, p, f] = dep[f, 0, x, :].astype(jnp.bfloat16)
            hsend[1, p, f] = dep[f, 3, x, :].astype(jnp.bfloat16)
        hsend[0, p, 4] = dep[0, 1, x, :].astype(jnp.bfloat16)
        hsend[1, p, 4] = dep[0, 2, x, :].astype(jnp.bfloat16)
        return 0

    lax.fori_loop(0, PIECES, pack, 0)
    pl.semaphore_wait(barrier, PIECES + 1)

    def start_halo(k, _):
        p = lax.rem(me + 1 + k, PIECES)
        halo(0, p).start()
        halo(1, p).start()
        return 0

    lax.fori_loop(0, PIECES, start_halo, 0)

    def nodes(p):
        halo(0, p).wait_recv()
        halo(1, p).wait_recv()
        x = cols(p)
        for f in range(4):
            low = dep[f, 1, x, :] + s_lo * hrecv[1, p, f].astype(jnp.float32)
            high = dep[f, 2, x, :] + s_hi * hrecv[0, p, f].astype(jnp.float32)
            nf[f, 0, x, :] = low
            nf[f, 1, x, :] = high
            rsend[p, f, 0] = low.astype(jnp.bfloat16)
            rsend[p, f, 1] = high.astype(jnp.bfloat16)
            if f == 0:
                xm = pl.ds(pl.multiple_of(p * COLS + 8, 8), COLS)
                mass[0, xm, :] = low
                mass[1, xm, :] = high
                below = s_lo * (hrecv[1, p, 4].astype(jnp.float32) + dep[0, 0, x, :])
                above = s_hi * (hrecv[0, p, 4].astype(jnp.float32) + dep[0, 3, x, :])
                gradz[0, x, :] = (high - below) * 0.5
                gradz[1, x, :] = (above - low) * 0.5

    def reduce_step(k, _):
        p = lax.rem(me + 1 + k, PIECES)
        nodes(p)
        share(p).start()
        return 0

    lax.fori_loop(0, PIECES - 1, reduce_step, 0)
    nodes(me)
    for z in range(2):
        mass[z, 7:8, :] = mass[z, 263:264, :]
        mass[z, 264:265, :] = mass[z, 8:9, :]

    def total_step(k, total):
        p = lax.rem(me + PIECES - 1 - k, PIECES)
        shared(p).wait_recv()
        return total + rrecv[p].astype(jnp.float32)

    total = lax.fori_loop(0, PIECES - 1, total_step, rsend[me].astype(jnp.float32))
    cbuf[me] = (total[1:] / jnp.maximum(total[0], MASS_FLOOR)).astype(jnp.bfloat16)

    def start_spread(k, _):
        spread(lax.rem(me + 1 + k, PIECES)).start()
        return 0

    lax.fori_loop(0, PIECES - 1, start_spread, 0)
    friction = fric[0]

    def finish(p):
        for z in range(2):
            x = cols(p)
            m = nf[0, z, x, :]
            gx = (mass[z, pl.ds(p * COLS + 9, COLS), :] - mass[z, pl.ds(p * COLS + 7, COLS), :]) * 0.5
            gy = (pltpu.roll(m, 127, 1) - pltpu.roll(m, 1, 1)) * 0.5
            gz = gradz[z, x, :]
            length = jnp.sqrt(gz * gz + gx * gx + gy * gy)
            inv = 1.0 / jnp.maximum(length, GRADIENT_FLOOR)
            normal = [gz * inv, gx * inv, gy * inv]
            inv_m = 1.0 / jnp.maximum(m, MASS_FLOOR)
            speed = [nf[1 + d, z, x, :] * inv_m for d in range(3)]
            rel = [speed[d] - cbuf[p, d, z].astype(jnp.float32) for d in range(3)]
            part = rel[0] * normal[0] + rel[1] * normal[1] + rel[2] * normal[2]
            approach = jnp.maximum(part, 0.0)
            tangent = [rel[d] - part * normal[d] for d in range(3)]
            slip = jnp.sqrt(tangent[0] * tangent[0] + tangent[1] * tangent[1] + tangent[2] * tangent[2])
            factor = jnp.minimum(friction * approach, slip) / jnp.maximum(slip, SLIP_FLOOR)
            flag = flags[z, x, :].astype(jnp.float32)
            for d in range(3):
                out[0, d, z, x, :] = speed[d] - flag * (approach * normal[d] + factor * tangent[d])

    finish(me)

    def finish_step(k, _):
        p = lax.rem(me + PIECES - 1 - k, PIECES)
        spreaded(p).wait_recv()
        finish(p)
        return 0

    lax.fori_loop(0, PIECES - 1, finish_step, 0)

    def drain(k, _):
        p = lax.rem(me + 1 + k, PIECES)
        share(p).wait_send()
        spread(p).wait_send()
        return 0

    lax.fori_loop(0, PIECES - 1, drain, 0)

    def drain_halo(p, _):
        halo(0, p).wait_send()
        halo(1, p).wait_send()
        return 0

    lax.fori_loop(0, PIECES, drain_halo, 0)


def exchange(friction, dep, flags):
    vm = pl.BlockSpec(memory_space=pltpu.VMEM)
    f32, bf = jnp.float32, jnp.bfloat16
    dma = pltpu.SemaphoreType.DMA
    return pl.pallas_call(
        comm_kernel,
        in_specs=[pl.BlockSpec(memory_space=pltpu.SMEM), vm, vm],
        out_specs=vm,
        out_shape=jax.ShapeDtypeStruct((1, 3, 2, 256, 128), f32),
        scratch_shapes=[
            pltpu.VMEM((2, PIECES, 5, COLS, 128), bf), pltpu.VMEM((2, PIECES, 5, COLS, 128), bf),
            pltpu.VMEM((4, 2, 256, 128), f32), pltpu.VMEM((2, 272, 128), f32),
            pltpu.VMEM((2, 256, 128), f32),
            pltpu.VMEM((PIECES, 4, 2, COLS, 128), bf), pltpu.VMEM((PIECES, 4, 2, COLS, 128), bf),
            pltpu.VMEM((PIECES, 3, 2, COLS, 128), bf),
            dma((2, PIECES)), dma((2, PIECES)), dma((PIECES,)), dma((PIECES,)), dma((PIECES,)), dma((PIECES,)),
        ],
        compiler_params=pltpu.CompilerParams(collective_id=0, has_side_effects=True, vmem_limit_bytes=40 << 20),
    )(friction, dep, flags)


def per_device(particle_mass, particle_velocity, spline_weights, particle_cells, block_counts, friction, contact_flags):
    dep = deposit((1, 0, 0), block_counts.reshape(32), particle_mass, particle_velocity, spline_weights, particle_cells)
    return exchange(friction, dep, contact_flags)


def solution(mesh):
    return jax.shard_map(
        per_device,
        mesh=mesh,
        in_specs=(
            P("mat", "gz"),
            P("mat", None, "gz"),
            P("mat", None, "gz"),
            P("mat", "gz"),
            P("mat", "gz", None),
            P("mat"),
            P("gz", None, None),
        ),
        out_specs=P("mat", None, "gz", None, None),
        check_vma=False,
    )
```

```python
import functools
import jax, jax.numpy as jnp
from jax import lax
from jax.sharding import PartitionSpec as P
from jax.experimental import pallas as pl
from jax.experimental.pallas import tpu as pltpu

BLOCKS=32; SLOTS=4096; W=32
ROWS=SLOTS//128
F32=jnp.float32; BF=jnp.bfloat16

def rows_const(n, fn, k):
    r = lax.broadcasted_iota(jnp.int32, (n, k), 0)
    return fn(r).astype(F32).astype(BF)

def dep_kernel(cfg, counts, mass_h, vel_h, wt_h, cells_h, out, mass, vel, wt, cells, acc, tbuf, lbuf, rbuf, prod, sems):
    UR, U, PARTS, skip, UF = cfg
    UNIT = UR * 128
    NCH = UR * U // 2
    PB = BLOCKS // PARTS
    PR = PB * ROWS
    def copies(q):
        r = pl.ds(q * PR, PR)
        return [pltpu.make_async_copy(mass_h.at[r], mass.at[r], sems.at[0, q]),
                pltpu.make_async_copy(vel_h.at[:, r], vel.at[:, r], sems.at[1, q]),
                pltpu.make_async_copy(wt_h.at[:, r], wt.at[:, r], sems.at[2, q]),
                pltpu.make_async_copy(cells_h.at[r], cells.at[r], sems.at[3, q])]
    for q in range(PARTS):
        for c in copies(q):
            c.start()
    ycon = [rows_const(W, lambda r, t=t: r - t, 128) for t in range(3)]
    xcon = [rows_const(16, lambda r, p=p: (r - p + 1) & 15, 128) for p in range(3)]
    zero = jnp.zeros((), BF)
    sub = lax.broadcasted_iota(jnp.int32, (8, 128), 0)
    lane_lo = lax.broadcasted_iota(jnp.int32, (W, 128), 1) < 64
    usub = lax.broadcasted_iota(jnp.int32, (UR, 128), 0)
    place_id = usub * 128 + lax.broadcasted_iota(jnp.int32, (UR, 128), 1)
    odd = (usub & 1) == 1

    def clear(b, _):
        acc[b] = jnp.zeros(acc.shape[1:], F32)
        return 0
    lax.fori_loop(0, BLOCKS, clear, 0)
    lbuf[...] = jnp.zeros(lbuf.shape, BF)
    rbuf[...] = jnp.zeros(rbuf.shape, BF)
    prod[...] = jnp.zeros(prod.shape, F32)

    def bc(tile, r, rows):
        return jnp.broadcast_to(tile[r:r+1], (rows, 128)).astype(BF)

    def load(b, c):
        n = counts[b]
        left_n = n - c * UNIT
        rr = pl.ds(pl.multiple_of(b * ROWS + jnp.minimum(c, ROWS // UR - 1) * UR, UR), UR)
        cl = cells[rr, :]
        live = place_id < left_n
        m = jnp.where(live, mass[rr, :], 0.0)
        y = cl & 127
        first = jnp.broadcast_to(y[:, 0:1], (UR, 128)) & ~7
        up = jnp.concatenate([first[0:1]] + [first[i - 1:i] for i in range(1, UR)], 0)
        first = jnp.where(odd, up, first)
        yrel = y - first
        spread = jnp.where(live, yrel, 0)
        bases = [first[2*j, 0] for j in range(UR // 2)]
        u = ((cl >> 7) & 7).astype(F32)
        top = cl >= 1024
        car = [m] + [m * vel[k, rr, :] for k in range(3)]
        w = [wt[r, rr, :] for r in range(9)]
        zn = [jnp.where(top, 0.0, w[0]), jnp.where(top, w[0], w[1]),
              jnp.where(top, w[1], w[2]), jnp.where(top, w[2], 0.0)]
        return bases, spread, yrel.astype(F32), (u, car, zn, w)

    def sides(yrel, data, r):
        u, car, zn, w = data
        ub = bc(u, r, 16)
        xw = jnp.where(ub == xcon[0], bc(w[3], r, 16), zero)
        xw = jnp.where(ub == xcon[1], bc(w[4], r, 16), xw)
        xw = jnp.where(ub == xcon[2], bc(w[5], r, 16), xw)
        yb = bc(yrel, r, W)
        yw = jnp.where(yb == ycon[0], bc(w[6], r, W), zero)
        yw = jnp.where(yb == ycon[1], bc(w[7], r, W), yw)
        yw = jnp.where(yb == ycon[2], bc(w[8], r, W), yw)
        return [bc(zn[z], r, 16) * xw for z in range(4)], [bc(car[f], r, W) * yw for f in range(4)]
    def build(yrel, data, j, i):
        for k in range(2):
            ls, rs = sides(yrel, data, 2 * j + k)
            for z in range(4):
                lbuf[i, z * 16:(z + 1) * 16, k * 128:(k + 1) * 128] = ls[z]
            for f in range(4):
                rbuf[i, f * W:(f + 1) * W, k * 128:(k + 1) * 128] = rs[f]
    def multiply(i):
        left = lbuf[i]
        left = jnp.concatenate([left, left], 0)
        res = lax.dot_general(rbuf[i], left, (((1,), (1,)), ((), ())), preferred_element_type=F32)
        for h in range(2):
            prod[i, h] = jnp.where(lane_lo, res[2 * h * W:(2 * h + 1) * W], res[(2 * h + 1) * W:(2 * h + 2) * W])
    def accumulate(i, b, base):
        rows = pl.ds(pl.multiple_of(base, 8), W)
        for h in range(2):
            acc[b, h, rows, :] += prod[i, h]

    def units(b):
        return (counts[b] + (UNIT - 1)) // UNIT

    def part(q, pend):
        for c in copies(q):
            c.wait()
        last = q * PB + PB - 1
        total = lax.fori_loop(q * PB, q * PB + PB, lambda b, t: t + units(b), 0)
        def group(g, state):
            b, c, (older, old) = state
            for i in range(NCH):
                accumulate(i, *older[i])
            for i in range(NCH):
                multiply(i)
            new = []
            far = None
            items = []
            i = 0
            for _ in range(U):
                bases, spread, yrel, data = load(b, c)
                items.append((b, c))
                for j in range(UR // 2):
                    build(yrel, data, j, i)
                    new.append((b, bases[j]))
                    i += 1
                far = spread if far is None else jnp.maximum(far, spread)
                done = jnp.logical_and(c + 1 >= units(b), b < last)
                b, c = jnp.where(done, b + 1, b), jnp.where(done, 0, c + 1)
            @pl.when(jnp.max(far) >= 24)
            def _():
                def one(bb, cc):
                    bases, spread, yrel, data = load(bb, cc)
                    for j in range(UR // 2):
                        def window(off, _):
                            base = bases[j] + off * W
                            @pl.when(base < 130)
                            def _():
                                build(yrel - (off * W).astype(F32), data, j, NCH)
                                multiply(NCH)
                                accumulate(NCH, bb, base)
                            return 0
                        lax.fori_loop(1, 5, window, 0)
                for bb, cc in items:
                    one(bb, cc)
            return b, c, (old, tuple(new))
        _, _, pend = lax.fori_loop(0, (total + U - 1) // U, group, (q * PB, 0, pend))
        return pend
    if skip != 1:
        none = tuple((0, 0) for _ in range(NCH))
        older, old = lax.fori_loop(0, PARTS, part, (none, none))
        for i in range(NCH):
            accumulate(i, *older[i])
        for i in range(NCH):
            multiply(i)
        for i in range(NCH):
            accumulate(i, *old[i])
    else:
        for q in range(PARTS):
            for c in copies(q):
                c.wait()

    def finish(b0, _):
        for k in range(UF):
            b = b0 * UF + k
            for h in range(2):
                head = acc[b, h, 1:9] + jnp.where(sub == 0, acc[b, h, 129:137], 0.0)
                tail = acc[b, h, 121:129] + jnp.where(sub == 7, jnp.broadcast_to(acc[b, h, 0:1], (8, 128)), 0.0)
                tbuf[b, h] = jnp.concatenate([head, acc[b, h, 9:121], tail], 0).T
        return 0
    if skip != 2:
        lax.fori_loop(0, BLOCKS // UF, finish, 0)
    def seams(b, _):
        here = pl.ds(pl.multiple_of(b * 8, 8), 8)
        dn = (b + BLOCKS - 1) & (BLOCKS - 1)
        up = (b + 1) & (BLOCKS - 1)
        for f in range(4):
            for z in range(4):
                o = (f % 2) * 64 + z * 16
                out[f, z, here, :] = (tbuf[b, f // 2, o:o + 8]
                    + jnp.where(sub == 0, tbuf[dn, f // 2, o + 8:o + 16], 0.0)
                    + jnp.where(sub == 7, tbuf[up, f // 2, o + 8:o + 16], 0.0))
        return 0
    if skip != 3:
        lax.fori_loop(0, BLOCKS, seams, 0)

def deposit(cfg, counts, mass, vel, wt, cells):
    UR, U, PARTS, skip, UF = cfg
    NCH = UR * U // 2
    hbm = pl.BlockSpec(memory_space=pltpu.MemorySpace.HBM)
    return pl.pallas_call(
        functools.partial(dep_kernel, cfg),
        in_specs=[pl.BlockSpec(memory_space=pltpu.SMEM), hbm, hbm, hbm, hbm],
        out_specs=pl.BlockSpec(memory_space=pltpu.VMEM),
        out_shape=jax.ShapeDtypeStruct((4, 4, 256, 128), F32),
        scratch_shapes=[pltpu.VMEM((1024, 128), F32), pltpu.VMEM((3, 1024, 128), F32), pltpu.VMEM((9, 1024, 128), F32),
                        pltpu.VMEM((1024, 128), jnp.int32), pltpu.VMEM((32, 2, 160, 128), F32),
                        pltpu.VMEM((32, 2, 128, 128), F32),
                        pltpu.VMEM((NCH + 1, 64, 256), BF), pltpu.VMEM((NCH + 1, 4 * W, 256), BF), pltpu.VMEM((NCH + 1, 2, W, 128), F32),
                        pltpu.SemaphoreType.DMA((4, PARTS))],
        compiler_params=pltpu.CompilerParams(vmem_limit_bytes=60 << 20),
    )(counts, mass.reshape(1024, 128), vel.reshape(3, 1024, 128), wt.reshape(9, 1024, 128), cells.reshape(1024, 128))

MASS_FLOOR = 0.2
GRADIENT_FLOOR = 0.1
SLIP_FLOOR = 0.05
PIECES = 8
COLS = 32
MESH = pl.DeviceIdType.MESH


def comm_kernel(fric, dep, flags, out, hsend, hrecv, nf, mass, gradz, rsend, rrecv, cbuf,
                h_ss, h_rs, r_ss, r_rs, c_ss, c_rs):
    slabs = lax.axis_size("gz")
    g = lax.axis_index("gz")
    me = lax.axis_index("mat")
    lo = lax.rem(g + slabs - 1, slabs)
    hi = lax.rem(g + 1, slabs)
    s_lo = jnp.where(g == 0, 0.0, 1.0)
    s_hi = jnp.where(g == slabs - 1, 0.0, 1.0)

    barrier = pltpu.get_barrier_semaphore()
    for other in (lo, hi):
        pl.semaphore_signal(barrier, inc=1, device_id={"gz": other, "mat": me}, device_id_type=MESH)
    for k in range(1, PIECES):
        pl.semaphore_signal(barrier, inc=1, device_id={"gz": g, "mat": lax.rem(me + k, PIECES)},
                            device_id_type=MESH)

    def halo(side, p):
        return pltpu.make_async_remote_copy(
            src_ref=hsend.at[side, p], dst_ref=hrecv.at[side, p],
            send_sem=h_ss.at[side, p], recv_sem=h_rs.at[side, p],
            device_id={"gz": lo if side == 0 else hi, "mat": me}, device_id_type=MESH)

    def share(p):
        return pltpu.make_async_remote_copy(
            src_ref=rsend.at[p], dst_ref=rrecv.at[me], send_sem=r_ss.at[p], recv_sem=r_rs.at[me],
            device_id={"gz": g, "mat": p}, device_id_type=MESH)

    def shared(p):
        return pltpu.make_async_remote_copy(
            src_ref=rsend.at[p], dst_ref=rrecv.at[p], send_sem=r_ss.at[p], recv_sem=r_rs.at[p],
            device_id={"gz": g, "mat": p}, device_id_type=MESH)

    def spread(p):
        return pltpu.make_async_remote_copy(
            src_ref=cbuf.at[me], dst_ref=cbuf.at[me], send_sem=c_ss.at[p], recv_sem=c_rs.at[me],
            device_id={"gz": g, "mat": p}, device_id_type=MESH)

    def spreaded(p):
        return pltpu.make_async_remote_copy(
            src_ref=cbuf.at[p], dst_ref=cbuf.at[p], send_sem=c_ss.at[p], recv_sem=c_rs.at[p],
            device_id={"gz": g, "mat": p}, device_id_type=MESH)

    def cols(p):
        return pl.ds(pl.multiple_of(p * COLS, COLS), COLS)

    def pack(k, _):
        p = lax.rem(me + 1 + k, PIECES)
        x = cols(p)
        for f in range(4):
            hsend[0, p, f] = dep[f, 0, x, :].astype(jnp.bfloat16)
            hsend[1, p, f] = dep[f, 3, x, :].astype(jnp.bfloat16)
        hsend[0, p, 4] = dep[0, 1, x, :].astype(jnp.bfloat16)
        hsend[1, p, 4] = dep[0, 2, x, :].astype(jnp.bfloat16)
        return 0

    lax.fori_loop(0, PIECES, pack, 0)
    pl.semaphore_wait(barrier, PIECES + 1)

    def start_halo(k, _):
        p = lax.rem(me + 1 + k, PIECES)
        halo(0, p).start()
        halo(1, p).start()
        return 0

    lax.fori_loop(0, PIECES, start_halo, 0)

    def nodes(p):
        halo(0, p).wait_recv()
        halo(1, p).wait_recv()
        x = cols(p)
        for f in range(4):
            low = dep[f, 1, x, :] + s_lo * hrecv[1, p, f].astype(jnp.float32)
            high = dep[f, 2, x, :] + s_hi * hrecv[0, p, f].astype(jnp.float32)
            nf[f, 0, x, :] = low
            nf[f, 1, x, :] = high
            rsend[p, f, 0] = low.astype(jnp.bfloat16)
            rsend[p, f, 1] = high.astype(jnp.bfloat16)
            if f == 0:
                xm = pl.ds(pl.multiple_of(p * COLS + 8, 8), COLS)
                mass[0, xm, :] = low
                mass[1, xm, :] = high
                below = s_lo * (hrecv[1, p, 4].astype(jnp.float32) + dep[0, 0, x, :])
                above = s_hi * (hrecv[0, p, 4].astype(jnp.float32) + dep[0, 3, x, :])
                gradz[0, x, :] = (high - below) * 0.5
                gradz[1, x, :] = (above - low) * 0.5

    def reduce_step(k, _):
        p = lax.rem(me + 1 + k, PIECES)
        nodes(p)
        share(p).start()
        return 0

    lax.fori_loop(0, PIECES - 1, reduce_step, 0)
    nodes(me)
    for z in range(2):
        mass[z, 7:8, :] = mass[z, 263:264, :]
        mass[z, 264:265, :] = mass[z, 8:9, :]

    def total_step(k, total):
        p = lax.rem(me + PIECES - 1 - k, PIECES)
        shared(p).wait_recv()
        return total + rrecv[p].astype(jnp.float32)

    total = lax.fori_loop(0, PIECES - 1, total_step, rsend[me].astype(jnp.float32))
    cbuf[me] = (total[1:] / jnp.maximum(total[0], MASS_FLOOR)).astype(jnp.bfloat16)

    def start_spread(k, _):
        spread(lax.rem(me + 1 + k, PIECES)).start()
        return 0

    lax.fori_loop(0, PIECES - 1, start_spread, 0)
    friction = fric[0]

    def finish(p):
        for z in range(2):
            x = cols(p)
            m = nf[0, z, x, :]
            gx = (mass[z, pl.ds(p * COLS + 9, COLS), :] - mass[z, pl.ds(p * COLS + 7, COLS), :]) * 0.5
            gy = (pltpu.roll(m, 127, 1) - pltpu.roll(m, 1, 1)) * 0.5
            gz = gradz[z, x, :]
            length = jnp.sqrt(gz * gz + gx * gx + gy * gy)
            inv = 1.0 / jnp.maximum(length, GRADIENT_FLOOR)
            normal = [gz * inv, gx * inv, gy * inv]
            inv_m = 1.0 / jnp.maximum(m, MASS_FLOOR)
            speed = [nf[1 + d, z, x, :] * inv_m for d in range(3)]
            rel = [speed[d] - cbuf[p, d, z].astype(jnp.float32) for d in range(3)]
            part = rel[0] * normal[0] + rel[1] * normal[1] + rel[2] * normal[2]
            approach = jnp.maximum(part, 0.0)
            tangent = [rel[d] - part * normal[d] for d in range(3)]
            slip = jnp.sqrt(tangent[0] * tangent[0] + tangent[1] * tangent[1] + tangent[2] * tangent[2])
            factor = jnp.minimum(friction * approach, slip) / jnp.maximum(slip, SLIP_FLOOR)
            flag = flags[z, x, :].astype(jnp.float32)
            for d in range(3):
                out[0, d, z, x, :] = speed[d] - flag * (approach * normal[d] + factor * tangent[d])

    finish(me)

    def finish_step(k, _):
        p = lax.rem(me + PIECES - 1 - k, PIECES)
        spreaded(p).wait_recv()
        finish(p)
        return 0

    lax.fori_loop(0, PIECES - 1, finish_step, 0)

    def drain(k, _):
        p = lax.rem(me + 1 + k, PIECES)
        share(p).wait_send()
        spread(p).wait_send()
        return 0

    lax.fori_loop(0, PIECES - 1, drain, 0)

    def drain_halo(p, _):
        halo(0, p).wait_send()
        halo(1, p).wait_send()
        return 0

    lax.fori_loop(0, PIECES, drain_halo, 0)


def exchange(friction, dep, flags):
    vm = pl.BlockSpec(memory_space=pltpu.VMEM)
    f32, bf = jnp.float32, jnp.bfloat16
    dma = pltpu.SemaphoreType.DMA
    return pl.pallas_call(
        comm_kernel,
        in_specs=[pl.BlockSpec(memory_space=pltpu.SMEM), vm, vm],
        out_specs=vm,
        out_shape=jax.ShapeDtypeStruct((1, 3, 2, 256, 128), f32),
        scratch_shapes=[
            pltpu.VMEM((2, PIECES, 5, COLS, 128), bf), pltpu.VMEM((2, PIECES, 5, COLS, 128), bf),
            pltpu.VMEM((4, 2, 256, 128), f32), pltpu.VMEM((2, 272, 128), f32),
            pltpu.VMEM((2, 256, 128), f32),
            pltpu.VMEM((PIECES, 4, 2, COLS, 128), bf), pltpu.VMEM((PIECES, 4, 2, COLS, 128), bf),
            pltpu.VMEM((PIECES, 3, 2, COLS, 128), bf),
            dma((2, PIECES)), dma((2, PIECES)), dma((PIECES,)), dma((PIECES,)), dma((PIECES,)), dma((PIECES,)),
        ],
        compiler_params=pltpu.CompilerParams(collective_id=0, has_side_effects=True, vmem_limit_bytes=40 << 20),
    )(friction, dep, flags)


def per_device(particle_mass, particle_velocity, spline_weights, particle_cells, block_counts, friction, contact_flags):
    dep = deposit((4, 8, 2, 0, 4), block_counts.reshape(32), particle_mass, particle_velocity, spline_weights, particle_cells)
    return exchange(friction, dep, contact_flags)


def solution(mesh):
    return jax.shard_map(
        per_device,
        mesh=mesh,
        in_specs=(
            P("mat", "gz"),
            P("mat", None, "gz"),
            P("mat", None, "gz"),
            P("mat", "gz"),
            P("mat", "gz", None),
            P("mat"),
            P("gz", None, None),
        ),
        out_specs=P("mat", None, "gz", None, None),
        check_vma=False,
    )
```

```python
import functools
import jax, jax.numpy as jnp
from jax import lax
from jax.sharding import PartitionSpec as P
from jax.experimental import pallas as pl
from jax.experimental.pallas import tpu as pltpu

BLOCKS=32; SLOTS=4096; W=32
ROWS=SLOTS//128
F32=jnp.float32; BF=jnp.bfloat16

def rows_const(n, fn, k):
    r = lax.broadcasted_iota(jnp.int32, (n, k), 0)
    return fn(r).astype(F32).astype(BF)

def dep_kernel(cfg, counts, mass_h, vel_h, wt_h, cells_h, out, mass, vel, wt, cells, acc, tbuf, lbuf, rbuf, prod, sems, obuf, osem):
    UR, U, HEAD, skip, UF, MODE = cfg
    UNIT = UR * 128
    NCH = UR * U // 2
    spans = [(0, HEAD), (HEAD, BLOCKS)]
    def copies(q):
        r = pl.ds(spans[q][0] * ROWS, (spans[q][1] - spans[q][0]) * ROWS)
        return [pltpu.make_async_copy(mass_h.at[r], mass.at[r], sems.at[0, q]),
                pltpu.make_async_copy(vel_h.at[:, r], vel.at[:, r], sems.at[1, q]),
                pltpu.make_async_copy(wt_h.at[:, r], wt.at[:, r], sems.at[2, q]),
                pltpu.make_async_copy(cells_h.at[r], cells.at[r], sems.at[3, q])]
    for q in range(2):
        for c in copies(q):
            c.start()
    ycon = [rows_const(W, lambda r, t=t: r - t, 128) for t in range(3)]
    xcon = [rows_const(16, lambda r, p=p: (r - p + 1) & 15, 128) for p in range(3)]
    zero = jnp.zeros((), BF)
    sub = lax.broadcasted_iota(jnp.int32, (8, 128), 0)
    lane_lo = lax.broadcasted_iota(jnp.int32, (W, 128), 1) < 64
    usub = lax.broadcasted_iota(jnp.int32, (UR, 128), 0)
    place_id = usub * 128 + lax.broadcasted_iota(jnp.int32, (UR, 128), 1)
    odd = (usub & 1) == 1

    def clear(b, _):
        acc[b] = jnp.zeros(acc.shape[1:], F32)
        return 0
    lax.fori_loop(0, BLOCKS, clear, 0)
    lbuf[...] = jnp.zeros(lbuf.shape, BF)
    rbuf[...] = jnp.zeros(rbuf.shape, BF)
    prod[...] = jnp.zeros(prod.shape, F32)

    def bc(tile, r, rows):
        return jnp.broadcast_to(tile[r:r+1], (rows, 128)).astype(BF)

    def load(b, c):
        n = counts[b]
        left_n = n - c * UNIT
        rr = pl.ds(pl.multiple_of(b * ROWS + jnp.minimum(c, ROWS // UR - 1) * UR, UR), UR)
        cl = cells[rr, :]
        live = place_id < left_n
        m = jnp.where(live, mass[rr, :], 0.0)
        y = cl & 127
        first = jnp.broadcast_to(y[:, 0:1], (UR, 128)) & ~7
        up = jnp.concatenate([first[0:1]] + [first[i - 1:i] for i in range(1, UR)], 0)
        first = jnp.where(odd, up, first)
        yrel = y - first
        spread = jnp.where(live, yrel, 0)
        bases = [first[2*j, 0] for j in range(UR // 2)]
        u = ((cl >> 7) & 7).astype(F32)
        top = cl >= 1024
        car = [m] + [m * vel[k, rr, :] for k in range(3)]
        w = [wt[r, rr, :] for r in range(9)]
        zn = [jnp.where(top, 0.0, w[0]), jnp.where(top, w[0], w[1]),
              jnp.where(top, w[1], w[2]), jnp.where(top, w[2], 0.0)]
        return bases, spread, yrel.astype(F32), (u, car, zn, w)

    def sides(yrel, data, r):
        u, car, zn, w = data
        ub = bc(u, r, 16)
        xw = jnp.where(ub == xcon[0], bc(w[3], r, 16), zero)
        xw = jnp.where(ub == xcon[1], bc(w[4], r, 16), xw)
        xw = jnp.where(ub == xcon[2], bc(w[5], r, 16), xw)
        yb = bc(yrel, r, W)
        yw = jnp.where(yb == ycon[0], bc(w[6], r, W), zero)
        yw = jnp.where(yb == ycon[1], bc(w[7], r, W), yw)
        yw = jnp.where(yb == ycon[2], bc(w[8], r, W), yw)
        return [bc(zn[z], r, 16) * xw for z in range(4)], [bc(car[f], r, W) * yw for f in range(4)]
    def build(yrel, data, j, i):
        for k in range(2):
            ls, rs = sides(yrel, data, 2 * j + k)
            for z in range(4):
                lbuf[i, z * 16:(z + 1) * 16, k * 128:(k + 1) * 128] = ls[z]
            for f in range(4):
                rbuf[i, f * W:(f + 1) * W, k * 128:(k + 1) * 128] = rs[f]
    def multiply(i, where=None):
        left = lbuf[i]
        left = jnp.concatenate([left, left], 0)
        res = lax.dot_general(rbuf[i], left, (((1,), (1,)), ((), ())), preferred_element_type=F32)
        for h in range(2):
            both = jnp.where(lane_lo, res[2 * h * W:(2 * h + 1) * W], res[(2 * h + 1) * W:(2 * h + 2) * W])
            if where is None:
                prod[i, h] = both
            else:
                acc[where[0], h, pl.ds(pl.multiple_of(where[1], 8), W), :] += both
    def accumulate(i, b, base):
        rows = pl.ds(pl.multiple_of(base, 8), W)
        for h in range(2):
            acc[b, h, rows, :] += prod[i, h]

    def units(b):
        return (counts[b] + (UNIT - 1)) // UNIT

    def part(q, pend):
        first_block = jnp.where(q == 0, 0, HEAD)
        last = jnp.where(q == 0, HEAD, BLOCKS) - 1
        @pl.when(q == 0)
        def _():
            for c in copies(0):
                c.wait()
        @pl.when(q == 1)
        def _():
            for c in copies(1):
                c.wait()
        total = lax.fori_loop(first_block, last + 1, lambda b, t: t + units(b), 0)
        def group(g, state):
            b, c, (older, old) = state
            new = []
            far = None
            items = []
            i = 0
            if MODE == 0:
                for i in range(NCH):
                    accumulate(i, *older[i])
                for i in range(NCH):
                    multiply(i)
            i = 0
            for _ in range(U):
                if MODE == 1:
                    for j in range(UR // 2):
                        accumulate(i + j, *older[i + j])
                        multiply(i + j)
                if MODE == 2:
                    for j in range(UR // 2):
                        multiply(i + j, old[i + j])
                bases, spread, yrel, data = load(b, c)
                items.append((b, c))
                for j in range(UR // 2):
                    build(yrel, data, j, i)
                    new.append((b, bases[j]))
                    i += 1
                far = spread if far is None else jnp.maximum(far, spread)
                done = jnp.logical_and(c + 1 >= units(b), b < last)
                b, c = jnp.where(done, b + 1, b), jnp.where(done, 0, c + 1)
            @pl.when(jnp.max(far) >= 24)
            def _():
                def one(bb, cc):
                    bases, spread, yrel, data = load(bb, cc)
                    for j in range(UR // 2):
                        def window(off, _):
                            base = bases[j] + off * W
                            @pl.when(base < 130)
                            def _():
                                build(yrel - (off * W).astype(F32), data, j, NCH)
                                multiply(NCH)
                                accumulate(NCH, bb, base)
                            return 0
                        lax.fori_loop(1, 5, window, 0)
                for bb, cc in items:
                    one(bb, cc)
            return b, c, (old, tuple(new))
        _, _, pend = lax.fori_loop(0, (total + U - 1) // U, group, (first_block, 0, pend))
        return pend
    if skip != 1:
        none = tuple((0, 0) for _ in range(NCH))
        older, old = lax.fori_loop(0, 2, part, (none, none))
        if MODE == 2:
            for i in range(NCH):
                multiply(i, old[i])
        else:
            for i in range(NCH):
                accumulate(i, *older[i])
            for i in range(NCH):
                multiply(i)
            for i in range(NCH):
                accumulate(i, *old[i])
    else:
        for q in range(2):
            for c in copies(q):
                c.wait()

    def finish(b0, _):
        for k in range(UF):
            b = b0 * UF + k
            for h in range(2):
                head = acc[b, h, 1:9] + jnp.where(sub == 0, acc[b, h, 129:137], 0.0)
                tail = acc[b, h, 121:129] + jnp.where(sub == 7, jnp.broadcast_to(acc[b, h, 0:1], (8, 128)), 0.0)
                tbuf[b, h] = jnp.concatenate([head, acc[b, h, 9:121], tail], 0).T
        return 0
    if skip != 2:
        lax.fori_loop(0, BLOCKS // UF, finish, 0)
    def piece(p):
        return pltpu.make_async_copy(obuf.at[p], out.at[p], osem.at[p])
    def seams(p, _):
        for j in range(4):
            b = p * 4 + j
            dn = (b + BLOCKS - 1) & (BLOCKS - 1)
            up = (b + 1) & (BLOCKS - 1)
            for k in range(16):
                o = (k // 4 % 2) * 64 + k % 4 * 16
                h = k // 8
                obuf[p, k, 8 * j:8 * j + 8, :] = (tbuf[b, h, o:o + 8]
                    + jnp.where(sub == 0, tbuf[dn, h, o + 8:o + 16], 0.0)
                    + jnp.where(sub == 7, tbuf[up, h, o + 8:o + 16], 0.0))
        piece(p).start()
        return 0
    if skip != 3:
        lax.fori_loop(0, 8, seams, 0)
        def drain(p, _):
            piece(p).wait()
            return 0
        lax.fori_loop(0, 8, drain, 0)

def deposit(cfg, counts, mass, vel, wt, cells):
    UR, U, HEAD, skip, UF, MODE = cfg
    NCH = UR * U // 2
    hbm = pl.BlockSpec(memory_space=pltpu.MemorySpace.HBM)
    return pl.pallas_call(
        functools.partial(dep_kernel, cfg),
        in_specs=[pl.BlockSpec(memory_space=pltpu.SMEM), hbm, hbm, hbm, hbm],
        out_specs=hbm,
        out_shape=jax.ShapeDtypeStruct((8, 16, 32, 128), F32),
        scratch_shapes=[pltpu.VMEM((1024, 128), F32), pltpu.VMEM((3, 1024, 128), F32), pltpu.VMEM((9, 1024, 128), F32),
                        pltpu.VMEM((1024, 128), jnp.int32), pltpu.VMEM((32, 2, 160, 128), F32),
                        pltpu.VMEM((32, 2, 128, 128), F32),
                        pltpu.VMEM((NCH + 1, 64, 256), BF), pltpu.VMEM((NCH + 1, 4 * W, 256), BF), pltpu.VMEM((NCH + 1, 2, W, 128), F32),
                        pltpu.SemaphoreType.DMA((4, 2)), pltpu.VMEM((8, 16, 32, 128), F32), pltpu.SemaphoreType.DMA((8,))],
        compiler_params=pltpu.CompilerParams(vmem_limit_bytes=60 << 20),
    )(counts, mass.reshape(1024, 128), vel.reshape(3, 1024, 128), wt.reshape(9, 1024, 128), cells.reshape(1024, 128))

MASS_FLOOR = 0.2
GRADIENT_FLOOR = 0.1
SLIP_FLOOR = 0.05
PIECES = 8
COLS = 32
MESH = pl.DeviceIdType.MESH


def comm_kernel(fric, dep_h, flags_h, out, dep, flags, obuf, d_s, f_s, o_s, hsend, hrecv, nf, mass, gradz, rsend, rrecv, cbuf,
                h_ss, h_rs, r_ss, r_rs, c_ss, c_rs):
    slabs = lax.axis_size("gz")
    g = lax.axis_index("gz")
    me = lax.axis_index("mat")
    lo = lax.rem(g + slabs - 1, slabs)
    hi = lax.rem(g + 1, slabs)
    s_lo = jnp.where(g == 0, 0.0, 1.0)
    s_hi = jnp.where(g == slabs - 1, 0.0, 1.0)

    def fetch(p):
        return pltpu.make_async_copy(dep_h.at[p], dep.at[p], d_s.at[p])

    def start_fetch(k, _):
        fetch(lax.rem(me + 1 + k, PIECES)).start()
        return 0

    lax.fori_loop(0, PIECES, start_fetch, 0)
    fetch_flags = pltpu.make_async_copy(flags_h, flags, f_s)
    fetch_flags.start()

    barrier = pltpu.get_barrier_semaphore()
    for other in (lo, hi):
        pl.semaphore_signal(barrier, inc=1, device_id={"gz": other, "mat": me}, device_id_type=MESH)
    for k in range(1, PIECES):
        pl.semaphore_signal(barrier, inc=1, device_id={"gz": g, "mat": lax.rem(me + k, PIECES)},
                            device_id_type=MESH)

    def halo(side, p):
        return pltpu.make_async_remote_copy(
            src_ref=hsend.at[side, p], dst_ref=hrecv.at[side, p],
            send_sem=h_ss.at[side, p], recv_sem=h_rs.at[side, p],
            device_id={"gz": lo if side == 0 else hi, "mat": me}, device_id_type=MESH)

    def share(p):
        return pltpu.make_async_remote_copy(
            src_ref=rsend.at[p], dst_ref=rrecv.at[me], send_sem=r_ss.at[p], recv_sem=r_rs.at[me],
            device_id={"gz": g, "mat": p}, device_id_type=MESH)

    def shared(p):
        return pltpu.make_async_remote_copy(
            src_ref=rsend.at[p], dst_ref=rrecv.at[p], send_sem=r_ss.at[p], recv_sem=r_rs.at[p],
            device_id={"gz": g, "mat": p}, device_id_type=MESH)

    def spread(p):
        return pltpu.make_async_remote_copy(
            src_ref=cbuf.at[me], dst_ref=cbuf.at[me], send_sem=c_ss.at[p], recv_sem=c_rs.at[me],
            device_id={"gz": g, "mat": p}, device_id_type=MESH)

    def spreaded(p):
        return pltpu.make_async_remote_copy(
            src_ref=cbuf.at[p], dst_ref=cbuf.at[p], send_sem=c_ss.at[p], recv_sem=c_rs.at[p],
            device_id={"gz": g, "mat": p}, device_id_type=MESH)

    def cols(p):
        return pl.ds(pl.multiple_of(p * COLS, COLS), COLS)

    def pack(k, _):
        p = lax.rem(me + 1 + k, PIECES)
        fetch(p).wait()
        for f in range(4):
            hsend[0, p, f] = dep[p, 4 * f + 0].astype(jnp.bfloat16)
            hsend[1, p, f] = dep[p, 4 * f + 3].astype(jnp.bfloat16)
        hsend[0, p, 4] = dep[p, 1].astype(jnp.bfloat16)
        hsend[1, p, 4] = dep[p, 2].astype(jnp.bfloat16)
        return 0

    lax.fori_loop(0, PIECES, pack, 0)
    pl.semaphore_wait(barrier, PIECES + 1)

    def start_halo(k, _):
        p = lax.rem(me + 1 + k, PIECES)
        halo(0, p).start()
        halo(1, p).start()
        return 0

    lax.fori_loop(0, PIECES, start_halo, 0)

    def nodes(p):
        halo(0, p).wait_recv()
        halo(1, p).wait_recv()
        x = cols(p)
        for f in range(4):
            low = dep[p, 4 * f + 1] + s_lo * hrecv[1, p, f].astype(jnp.float32)
            high = dep[p, 4 * f + 2] + s_hi * hrecv[0, p, f].astype(jnp.float32)
            nf[f, 0, x, :] = low
            nf[f, 1, x, :] = high
            rsend[p, f, 0] = low.astype(jnp.bfloat16)
            rsend[p, f, 1] = high.astype(jnp.bfloat16)
            if f == 0:
                xm = pl.ds(pl.multiple_of(p * COLS + 8, 8), COLS)
                mass[0, xm, :] = low
                mass[1, xm, :] = high
                below = s_lo * (hrecv[1, p, 4].astype(jnp.float32) + dep[p, 0])
                above = s_hi * (hrecv[0, p, 4].astype(jnp.float32) + dep[p, 3])
                gradz[0, x, :] = (high - below) * 0.5
                gradz[1, x, :] = (above - low) * 0.5

    def reduce_step(k, _):
        p = lax.rem(me + 1 + k, PIECES)
        nodes(p)
        share(p).start()
        return 0

    lax.fori_loop(0, PIECES - 1, reduce_step, 0)
    nodes(me)
    for z in range(2):
        mass[z, 7:8, :] = mass[z, 263:264, :]
        mass[z, 264:265, :] = mass[z, 8:9, :]

    def total_step(k, total):
        p = lax.rem(me + PIECES - 1 - k, PIECES)
        shared(p).wait_recv()
        return total + rrecv[p].astype(jnp.float32)

    total = lax.fori_loop(0, PIECES - 1, total_step, rsend[me].astype(jnp.float32))
    cbuf[me] = (total[1:] / jnp.maximum(total[0], MASS_FLOOR)).astype(jnp.bfloat16)

    def start_spread(k, _):
        spread(lax.rem(me + 1 + k, PIECES)).start()
        return 0

    lax.fori_loop(0, PIECES - 1, start_spread, 0)
    friction = fric[0]
    fetch_flags.wait()

    def result(p):
        return pltpu.make_async_copy(obuf.at[:, :, cols(p)], out.at[0, :, :, cols(p)], o_s.at[p])

    def finish(p):
        for z in range(2):
            x = cols(p)
            m = nf[0, z, x, :]
            gx = (mass[z, pl.ds(p * COLS + 9, COLS), :] - mass[z, pl.ds(p * COLS + 7, COLS), :]) * 0.5
            gy = (pltpu.roll(m, 127, 1) - pltpu.roll(m, 1, 1)) * 0.5
            gz = gradz[z, x, :]
            length = jnp.sqrt(gz * gz + gx * gx + gy * gy)
            inv = 1.0 / jnp.maximum(length, GRADIENT_FLOOR)
            normal = [gz * inv, gx * inv, gy * inv]
            inv_m = 1.0 / jnp.maximum(m, MASS_FLOOR)
            speed = [nf[1 + d, z, x, :] * inv_m for d in range(3)]
            rel = [speed[d] - cbuf[p, d, z].astype(jnp.float32) for d in range(3)]
            part = rel[0] * normal[0] + rel[1] * normal[1] + rel[2] * normal[2]
            approach = jnp.maximum(part, 0.0)
            tangent = [rel[d] - part * normal[d] for d in range(3)]
            slip = jnp.sqrt(tangent[0] * tangent[0] + tangent[1] * tangent[1] + tangent[2] * tangent[2])
            factor = jnp.minimum(friction * approach, slip) / jnp.maximum(slip, SLIP_FLOOR)
            flag = flags[z, x, :].astype(jnp.float32)
            for d in range(3):
                obuf[d, z, x, :] = speed[d] - flag * (approach * normal[d] + factor * tangent[d])

    finish(me)
    result(me).start()

    def finish_step(k, _):
        p = lax.rem(me + PIECES - 1 - k, PIECES)
        spreaded(p).wait_recv()
        finish(p)
        result(p).start()
        return 0

    lax.fori_loop(0, PIECES - 1, finish_step, 0)

    def drain(k, _):
        p = lax.rem(me + 1 + k, PIECES)
        share(p).wait_send()
        spread(p).wait_send()
        return 0

    lax.fori_loop(0, PIECES - 1, drain, 0)

    def drain_halo(p, _):
        halo(0, p).wait_send()
        halo(1, p).wait_send()
        result(p).wait()
        return 0

    lax.fori_loop(0, PIECES, drain_halo, 0)


def exchange(friction, dep, flags):
    hbm = pl.BlockSpec(memory_space=pltpu.MemorySpace.HBM)
    f32, bf = jnp.float32, jnp.bfloat16
    dma = pltpu.SemaphoreType.DMA
    return pl.pallas_call(
        comm_kernel,
        in_specs=[pl.BlockSpec(memory_space=pltpu.SMEM), hbm, hbm],
        out_specs=hbm,
        out_shape=jax.ShapeDtypeStruct((1, 3, 2, 256, 128), f32),
        scratch_shapes=[
            pltpu.VMEM((PIECES, 16, COLS, 128), f32), pltpu.VMEM((2, 256, 128), jnp.int32),
            pltpu.VMEM((3, 2, 256, 128), f32), dma((PIECES,)), dma, dma((PIECES,)),
            pltpu.VMEM((2, PIECES, 5, COLS, 128), bf), pltpu.VMEM((2, PIECES, 5, COLS, 128), bf),
            pltpu.VMEM((4, 2, 256, 128), f32), pltpu.VMEM((2, 272, 128), f32),
            pltpu.VMEM((2, 256, 128), f32),
            pltpu.VMEM((PIECES, 4, 2, COLS, 128), bf), pltpu.VMEM((PIECES, 4, 2, COLS, 128), bf),
            pltpu.VMEM((PIECES, 3, 2, COLS, 128), bf),
            dma((2, PIECES)), dma((2, PIECES)), dma((PIECES,)), dma((PIECES,)), dma((PIECES,)), dma((PIECES,)),
        ],
        compiler_params=pltpu.CompilerParams(collective_id=0, has_side_effects=True, vmem_limit_bytes=60 << 20),
    )(friction, dep, flags)


def per_device(particle_mass, particle_velocity, spline_weights, particle_cells, block_counts, friction, contact_flags):
    dep = deposit((4, 8, 4, 0, 4, 2), block_counts.reshape(32), particle_mass, particle_velocity, spline_weights, particle_cells)
    return exchange(friction, dep, contact_flags)


def solution(mesh):
    return jax.shard_map(
        per_device,
        mesh=mesh,
        in_specs=(
            P("mat", "gz"),
            P("mat", None, "gz"),
            P("mat", None, "gz"),
            P("mat", "gz"),
            P("mat", "gz", None),
            P("mat"),
            P("gz", None, None),
        ),
        out_specs=P("mat", None, "gz", None, None),
        check_vma=False,
    )
```

```python
import functools
import jax
import jax.numpy as jnp
from jax import lax
from jax.experimental import pallas as pl
from jax.experimental.pallas import tpu as pltpu
from jax.sharding import PartitionSpec as P

BLOCKS = 32
SLOTS = 4096
ROWS = SLOTS // 128
UR = 4
UNIT = UR * 128
PER_BLOCK = SLOTS // UNIT
W = 24
HEAD = 4
F32, BF = jnp.float32, jnp.bfloat16


def deposit_kernel(U, XP, ORDER, counts, mass_h, vel_h, wt_h, cells_h, out, mass, vel, wt, cells, acc, tbuf, prep,
                   lbuf, rbuf, obuf, urow, uleft, ubase, in_sem, out_sem):
    chunks = U * UR // 2

    def copies(q):
        first, count = ((0, HEAD), (HEAD, BLOCKS - HEAD))[q]
        r = pl.ds(first * ROWS, count * ROWS)
        return [pltpu.make_async_copy(mass_h.at[r], mass.at[r], in_sem.at[0, q]),
                pltpu.make_async_copy(vel_h.at[:, r], vel.at[:, r], in_sem.at[1, q]),
                pltpu.make_async_copy(wt_h.at[:, r], wt.at[:, r], in_sem.at[2, q]),
                pltpu.make_async_copy(cells_h.at[r], cells.at[r], in_sem.at[3, q])]

    for q in range(2):
        for c in copies(q):
            c.start()

    sub = lax.broadcasted_iota(jnp.int32, (8, 128), 0)
    usub = lax.broadcasted_iota(jnp.int32, (UR, 128), 0)
    place_id = usub * 128 + lax.broadcasted_iota(jnp.int32, (UR, 128), 1)
    odd = (usub & 1) == 1
    row16 = lax.broadcasted_iota(jnp.int32, (16, 128), 0)

    def const(values):
        return values.astype(F32).astype(BF)

    xcon = [const((row16 - p + 1) & 15) for p in range(3)]
    ycon = [const(row16 - t) for t in range(3)]
    ycon_b = [const(16 + (row16 & 7) - t) for t in range(3)]
    upper = const(row16) < jnp.asarray(8, BF)
    zero = jnp.zeros((), BF)

    def dead(i, row):
        urow[i] = row
        uleft[i] = 0

    for i in range(2 * U):
        dead(i, 0)
    for i in range(2 * chunks):
        ubase[i] = 0

    def list_block(b, at):
        n = counts[b]
        for c in range(PER_BLOCK):
            urow[at + c] = b * ROWS + c * UR
            uleft[at + c] = n - c * UNIT
        return at + (n + (UNIT - 1)) // UNIT

    head_end = lax.fori_loop(0, HEAD, list_block, 2 * U)
    end = lax.fori_loop(HEAD, BLOCKS, list_block, head_end)
    for i in range(3 * U):
        dead(end + i, BLOCKS * ROWS - UR)

    def clear(b, _):
        acc[b] = jnp.zeros(acc.shape[1:], F32)
        return 0

    lax.fori_loop(0, BLOCKS, clear, 0)
    prep[...] = jnp.zeros(prep.shape, F32)
    lbuf[...] = jnp.zeros(lbuf.shape, BF)
    rbuf[...] = jnp.zeros(rbuf.shape, BF)

    def prepare(slot, unit):
        row = urow[unit]
        rr = pl.ds(pl.multiple_of(row, UR), UR)
        cl = cells[rr, :]
        live = place_id < uleft[unit]
        m = jnp.where(live, mass[rr, :], 0.0)
        y = cl & 127
        first = jnp.broadcast_to(y[:, 0:1], (UR, 128)) & ~7
        before = jnp.concatenate([first[0:1]] + [first[i - 1:i] for i in range(1, UR)], 0)
        first = jnp.where(odd, before, first)
        yrel = y - first
        top = cl >= 1024
        w = [wt[a, rr, :] for a in range(3)]
        prep[slot, 0] = yrel.astype(F32)
        prep[slot, 1] = ((cl >> 7) & 7).astype(F32)
        prep[slot, 2] = m
        for d in range(3):
            prep[slot, 3 + d] = m * vel[d, rr, :]
        prep[slot, 6] = jnp.where(top, 0.0, w[0])
        prep[slot, 7] = jnp.where(top, w[0], w[1])
        prep[slot, 8] = jnp.where(top, w[1], w[2])
        prep[slot, 9] = jnp.where(top, w[2], 0.0)
        return [first[2 * j, 0] for j in range(UR // 2)], jnp.where(live, yrel, 0)

    def build(i, slot, unit, j):
        row = urow[unit]
        for k in range(2):
            r = 2 * j + k

            def wide(tile):
                return jnp.broadcast_to(tile, (16, 128)).astype(BF)

            def own(q):
                return wide(prep[slot, q, r:r + 1, :])

            def weight(q):
                return wide(wt[q, pl.ds(row + r, 1), :])

            def taps(index, con, w):
                tile = jnp.where(index == con[0], w[0], zero)
                tile = jnp.where(index == con[1], w[1], tile)
                return jnp.where(index == con[2], w[2], tile)

            lanes = slice(k * 128, (k + 1) * 128)
            xw = taps(own(1), xcon, [weight(3 + p) for p in range(3)])
            for z in range(4):
                lbuf[i, z * 16:(z + 1) * 16, lanes] = own(6 + z) * xw
            wy = [weight(6 + t) for t in range(3)]
            yb = own(0)
            ya, yz = taps(yb, ycon, wy), taps(yb, ycon_b, wy)
            cb = [own(2 + f) for f in range(4)]
            for f in range(4):
                rbuf[i, f * 16:(f + 1) * 16, lanes] = cb[f] * ya
            for h in range(2):
                rbuf[i, 64 + h * 16:80 + h * 16, lanes] = jnp.where(upper, cb[2 * h], cb[2 * h + 1]) * yz

    def multiply(i, b, base):
        res = lax.dot_general(rbuf[i], lbuf[i], (((1,), (1,)), ((), ())), preferred_element_type=F32)
        for f in range(4):
            acc[b, f, pl.ds(pl.multiple_of(base, 8), 16), 0:64] += res[16 * f:16 * f + 16]
            acc[b, f, pl.ds(pl.multiple_of(base + 16, 8), 8), 0:64] += res[64 + 8 * f:72 + 8 * f]

    def turn(b):
        for h in range(2):
            def rows(f):
                head = acc[b, f, 1:9] + jnp.where(sub == 0, acc[b, f, 129:137], 0.0)
                tail = acc[b, f, 121:129] + jnp.where(sub == 7, jnp.broadcast_to(acc[b, f, 0:1], (8, 128)), 0.0)
                return jnp.concatenate([head, acc[b, f, 9:121], tail], 0)
            tbuf[b, h] = (rows(2 * h) + pltpu.roll(rows(2 * h + 1), 64, 1)).T

    def group(g, state):
        t, far_before = state
        at = g * U
        more = jnp.max(far_before) >= W - 2
        far = None
        if XP and ORDER == 0:
            for k in range(XP):
                turn(jnp.minimum(t + k, BLOCKS - 1))
        for k in range(U):
            if XP and ORDER == 1 and k % (U // XP) == 0:
                turn(jnp.minimum(t + k // (U // XP), BLOCKS - 1))
            for j in range(UR // 2):
                i = k * (UR // 2) + j
                multiply(i, urow[at + k] // ROWS, ubase[2 * at + i])
                build(i, k, at + U + k, j)
            bases, spread = prepare(k, at + 2 * U + k)
            for j in range(UR // 2):
                ubase[2 * (at + 2 * U) + k * (UR // 2) + j] = bases[j]
            far = spread if far is None else jnp.maximum(far, spread)

        if XP:
            t = jnp.maximum(t, jnp.minimum(t + XP, urow[at] // ROWS))

        @pl.when(more)
        def _():
            def one(k, _):
                unit = at + U + k
                b = urow[unit] // ROWS
                prepare(U, unit)

                def window(off, _):
                    prep[U, 0] = prep[U, 0] - float(W)
                    for j in range(UR // 2):
                        base = ubase[2 * unit + j] + off * W

                        @pl.when(base < 130)
                        def _():
                            build(chunks, U, unit, j)
                            multiply(chunks, b, base)
                    return 0

                lax.fori_loop(1, 6, window, 0)
                return 0

            lax.fori_loop(0, U, one, 0)

        return t, far

    for c in copies(0):
        c.wait()
    head_groups = (head_end - 2 * U) // U
    state = lax.fori_loop(0, head_groups, group, (0, jnp.zeros((UR, 128), jnp.int32)))
    for c in copies(1):
        c.wait()
    t, _ = lax.fori_loop(head_groups, (end + U - 1) // U, group, state)

    def rest(k, _):
        for j in range(4):
            turn(jnp.minimum(t + 4 * k + j, BLOCKS - 1))
        return 0

    lax.fori_loop(0, (BLOCKS - t + 3) // 4, rest, 0)

    def piece(p):
        return pltpu.make_async_copy(obuf.at[p], out.at[p], out_sem.at[p])

    def seams(p, _):
        for j in range(4):
            b = p * 4 + j
            dn = (b + BLOCKS - 1) & (BLOCKS - 1)
            up = (b + 1) & (BLOCKS - 1)
            for k in range(16):
                o = (k // 4 % 2) * 64 + k % 4 * 16
                h = k // 8
                obuf[p, k, 8 * j:8 * j + 8, :] = (
                    tbuf[b, h, o:o + 8]
                    + jnp.where(sub == 0, tbuf[dn, h, o + 8:o + 16], 0.0)
                    + jnp.where(sub == 7, tbuf[up, h, o + 8:o + 16], 0.0))
        piece(p).start()
        return 0

    lax.fori_loop(0, 8, seams, 0)

    def drain_out(p, _):
        piece(p).wait()
        return 0

    lax.fori_loop(0, 8, drain_out, 0)


def deposit(cfg, counts, mass, vel, wt, cells):
    U, XP, ORDER = cfg
    chunks = U * UR // 2
    hbm = pl.BlockSpec(memory_space=pltpu.MemorySpace.HBM)
    units = BLOCKS * PER_BLOCK + 5 * U + PER_BLOCK
    return pl.pallas_call(
        functools.partial(deposit_kernel, U, XP, ORDER),
        in_specs=[pl.BlockSpec(memory_space=pltpu.SMEM), hbm, hbm, hbm, hbm],
        out_specs=hbm,
        out_shape=jax.ShapeDtypeStruct((112, 16, 32, 128), F32),
        scratch_shapes=[
            pltpu.VMEM((1024, 128), F32), pltpu.VMEM((3, 1024, 128), F32), pltpu.VMEM((9, 1024, 128), F32),
            pltpu.VMEM((1024, 128), jnp.int32), pltpu.VMEM((BLOCKS, 4, 160, 128), F32),
            pltpu.VMEM((BLOCKS, 2, 128, 128), F32), pltpu.VMEM((U + 1, 10, UR, 128), F32),
            pltpu.VMEM((chunks + 1, 64, 256), BF), pltpu.VMEM((chunks + 1, 4 * W, 256), BF),
            pltpu.VMEM((8, 16, 32, 128), F32),
            pltpu.SMEM((units,), jnp.int32), pltpu.SMEM((units,), jnp.int32), pltpu.SMEM((2 * units,), jnp.int32),
            pltpu.SemaphoreType.DMA((4, 2)), pltpu.SemaphoreType.DMA((8,)),
        ],
        compiler_params=pltpu.CompilerParams(vmem_limit_bytes=60 << 20),
    )(counts, mass.reshape(1024, 128), vel.reshape(3, 1024, 128), wt.reshape(9, 1024, 128), cells.reshape(1024, 128))


MASS_FLOOR = 0.2
GRADIENT_FLOOR = 0.1
SLIP_FLOOR = 0.05
PIECES = 8
COLS = 32
MID = 7
MESH = pl.DeviceIdType.MESH


def comm_kernel(fric, dep_h, flags_h, out, dep, flags, d_s, f_s, hsend, hrecv, msend, mrecv, nf, mass, rsend, rrecv, ysend,
                yrecv, cbuf, h_ss, h_rs, m_ss, m_rs, r_ss, r_rs, y_ss, y_rs, c_ss, c_rs):
    slabs = lax.axis_size("gz")
    g = lax.axis_index("gz")
    me = lax.axis_index("mat")
    lo = lax.rem(g + slabs - 1, slabs)
    hi = lax.rem(g + 1, slabs)
    s_lo = jnp.where(g == 0, 0.0, 1.0)
    s_hi = jnp.where(g == slabs - 1, 0.0, 1.0)

    def fetch(p):
        return pltpu.make_async_copy(dep_h.at[p], dep.at[p], d_s.at[p])

    def start_fetch(k, _):
        fetch(lax.rem(me + 1 + k, PIECES)).start()
        return 0

    lax.fori_loop(0, PIECES, start_fetch, 0)
    fetch_flags = pltpu.make_async_copy(flags_h, flags, f_s)
    fetch_flags.start()

    barrier = pltpu.get_barrier_semaphore()
    for other in (lo, hi):
        pl.semaphore_signal(barrier, inc=1, device_id={"gz": other, "mat": me}, device_id_type=MESH)
    for k in range(1, PIECES):
        pl.semaphore_signal(barrier, inc=1, device_id={"gz": g, "mat": lax.rem(me + k, PIECES)},
                            device_id_type=MESH)

    def halo(side, p):
        return pltpu.make_async_remote_copy(
            src_ref=hsend.at[side, p], dst_ref=hrecv.at[side, p],
            send_sem=h_ss.at[side, p], recv_sem=h_rs.at[side, p],
            device_id={"gz": lo if side == 0 else hi, "mat": me}, device_id_type=MESH)

    x_me = me // 2
    y_me = me % 2

    def order(k):
        return lax.rem(x_me + 1 + k, 4) * 2 + jnp.where(k < 4, 1 - y_me, y_me)

    def edge(side):
        return pltpu.make_async_remote_copy(
            src_ref=msend.at[side], dst_ref=mrecv.at[side], send_sem=m_ss.at[side], recv_sem=m_rs.at[side],
            device_id={"gz": lo if side == 0 else hi, "mat": me}, device_id_type=MESH)

    def share(k):
        half = k // 4
        return pltpu.make_async_remote_copy(
            src_ref=rsend.at[order(k)], dst_ref=rrecv.at[half, x_me], send_sem=r_ss.at[k],
            recv_sem=r_rs.at[half, x_me],
            device_id={"gz": g, "mat": lax.rem(x_me + 1 + k, 4) * 2 + y_me}, device_id_type=MESH)

    def shared(half, x):
        return pltpu.make_async_remote_copy(
            src_ref=rsend.at[0], dst_ref=rrecv.at[half, x], send_sem=r_ss.at[0], recv_sem=r_rs.at[half, x],
            device_id={"gz": g, "mat": x * 2 + y_me}, device_id_type=MESH)

    def cross():
        return pltpu.make_async_remote_copy(
            src_ref=ysend, dst_ref=yrecv, send_sem=y_ss, recv_sem=y_rs,
            device_id={"gz": g, "mat": x_me * 2 + 1 - y_me}, device_id_type=MESH)

    def spread(p):
        return pltpu.make_async_remote_copy(
            src_ref=cbuf.at[me], dst_ref=cbuf.at[me], send_sem=c_ss.at[p], recv_sem=c_rs.at[me],
            device_id={"gz": g, "mat": p}, device_id_type=MESH)

    def spreaded(p):
        return pltpu.make_async_remote_copy(
            src_ref=cbuf.at[p], dst_ref=cbuf.at[p], send_sem=c_ss.at[p], recv_sem=c_rs.at[p],
            device_id={"gz": g, "mat": p}, device_id_type=MESH)

    def cols(p):
        return pl.ds(pl.multiple_of(p * COLS, COLS), COLS)

    def pack(k, _):
        p = order(k)
        fetch(p).wait()
        for f in range(4):
            hsend[0, p, f] = dep[p, 4 * f + 0].astype(jnp.bfloat16)
            hsend[1, p, f] = dep[p, 4 * f + 3].astype(jnp.bfloat16)
        msend[0, cols(p), :] = dep[p, 1].astype(jnp.bfloat16)
        msend[1, cols(p), :] = dep[p, 2].astype(jnp.bfloat16)
        return 0

    lax.fori_loop(0, PIECES, pack, 0)
    pl.semaphore_wait(barrier, PIECES + 1)

    def start_halo(k, _):
        p = order(k)
        halo(0, p).start()
        halo(1, p).start()
        return 0

    lax.fori_loop(0, PIECES, start_halo, 0)
    edge(0).start()
    edge(1).start()

    def nodes(p):
        halo(0, p).wait_recv()
        halo(1, p).wait_recv()
        x = cols(p)
        for f in range(4):
            low = dep[p, 4 * f + 1] + s_lo * hrecv[1, p, f].astype(jnp.float32)
            high = dep[p, 4 * f + 2] + s_hi * hrecv[0, p, f].astype(jnp.float32)
            nf[f, 0, x, :] = low
            nf[f, 1, x, :] = high
            rsend[p, f, 0] = low.astype(jnp.bfloat16)
            rsend[p, f, 1] = high.astype(jnp.bfloat16)
            if f == 0:
                xm = pl.ds(pl.multiple_of(p * COLS + 8, 8), COLS)
                mass[0, xm, :] = low
                mass[1, xm, :] = high

    def reduce_step(k, _):
        nodes(order(k))
        share(k).start()
        return 0

    def total_step(half):
        def step(k, total):
            x = lax.rem(x_me + 3 - k, 4)
            shared(half, x).wait_recv()
            return total + rrecv[half, x].astype(jnp.float32)
        own = rsend[order(4 * half + 3)].astype(jnp.float32)
        return lax.fori_loop(0, 3, step, own)

    lax.fori_loop(0, 3, reduce_step, 0)
    nodes(order(3))
    lax.fori_loop(4, MID, reduce_step, 0)
    ysend[...] = total_step(0).astype(jnp.bfloat16)
    cross().start()
    lax.fori_loop(MID, 7, reduce_step, 0)
    nodes(me)
    for z in range(2):
        mass[z, 7:8, :] = mass[z, 263:264, :]
        mass[z, 264:265, :] = mass[z, 8:9, :]

    total = total_step(1)
    cross().wait_recv()
    total = total + yrecv[...].astype(jnp.float32)
    cbuf[me] = (total[1:] / jnp.maximum(total[0], MASS_FLOOR)).astype(jnp.bfloat16)

    def start_spread(k, _):
        spread(lax.rem(me + 1 + k, PIECES)).start()
        return 0

    lax.fori_loop(0, PIECES - 1, start_spread, 0)
    friction = fric[0]
    fetch_flags.wait()
    edge(0).wait_recv()
    edge(1).wait_recv()

    def finish(p):
        for z in range(2):
            x = cols(p)
            m = nf[0, z, x, :]
            gx = (mass[z, pl.ds(p * COLS + 9, COLS), :] - mass[z, pl.ds(p * COLS + 7, COLS), :]) * 0.5
            gy = (pltpu.roll(m, 127, 1) - pltpu.roll(m, 1, 1)) * 0.5
            if z == 0:
                below = s_lo * (mrecv[1, x, :].astype(jnp.float32) + dep[p, 0])
                gz = (nf[0, 1, x, :] - below) * 0.5
            else:
                above = s_hi * (mrecv[0, x, :].astype(jnp.float32) + dep[p, 3])
                gz = (above - nf[0, 0, x, :]) * 0.5
            length = jnp.sqrt(gz * gz + gx * gx + gy * gy)
            inv = 1.0 / jnp.maximum(length, GRADIENT_FLOOR)
            normal = [gz * inv, gx * inv, gy * inv]
            inv_m = 1.0 / jnp.maximum(m, MASS_FLOOR)
            speed = [nf[1 + d, z, x, :] * inv_m for d in range(3)]
            rel = [speed[d] - cbuf[p, d, z].astype(jnp.float32) for d in range(3)]
            part = rel[0] * normal[0] + rel[1] * normal[1] + rel[2] * normal[2]
            approach = jnp.maximum(part, 0.0)
            tangent = [rel[d] - part * normal[d] for d in range(3)]
            slip = jnp.sqrt(tangent[0] * tangent[0] + tangent[1] * tangent[1] + tangent[2] * tangent[2])
            factor = jnp.minimum(friction * approach, slip) / jnp.maximum(slip, SLIP_FLOOR)
            flag = flags[z, x, :].astype(jnp.float32)
            for d in range(3):
                out[0, d, z, x, :] = speed[d] - flag * (approach * normal[d] + factor * tangent[d])

    finish(me)
    def finish_step(k, _):
        p = lax.rem(me + PIECES - 1 - k, PIECES)
        spreaded(p).wait_recv()
        finish(p)
        return 0

    lax.fori_loop(0, PIECES - 1, finish_step, 0)

    def drain(k, _):
        p = lax.rem(me + 1 + k, PIECES)
        spread(p).wait_send()
        return 0

    lax.fori_loop(0, PIECES - 1, drain, 0)

    def drain_share(k, _):
        share(k).wait_send()
        share(k + 4).wait_send()
        return 0

    lax.fori_loop(0, 3, drain_share, 0)
    cross().wait_send()
    edge(0).wait_send()
    edge(1).wait_send()

    def drain_halo(p, _):
        halo(0, p).wait_send()
        halo(1, p).wait_send()
        return 0

    lax.fori_loop(0, PIECES, drain_halo, 0)


def exchange(friction, dep, flags):
    hbm = pl.BlockSpec(memory_space=pltpu.MemorySpace.HBM)
    f32, bf = jnp.float32, jnp.bfloat16
    dma = pltpu.SemaphoreType.DMA
    return pl.pallas_call(
        comm_kernel,
        in_specs=[pl.BlockSpec(memory_space=pltpu.SMEM), hbm, hbm],
        out_specs=pl.BlockSpec(memory_space=pltpu.VMEM),
        out_shape=jax.ShapeDtypeStruct((1, 3, 2, 256, 128), f32),
        scratch_shapes=[
            pltpu.VMEM((PIECES, 16, COLS, 128), f32), pltpu.VMEM((2, 256, 128), jnp.int32),
            dma((PIECES,)), dma,
            pltpu.VMEM((2, PIECES, 4, COLS, 128), bf), pltpu.VMEM((2, PIECES, 4, COLS, 128), bf),
            pltpu.VMEM((2, 256, 128), bf), pltpu.VMEM((2, 256, 128), bf),
            pltpu.VMEM((4, 2, 256, 128), f32), pltpu.VMEM((2, 272, 128), f32),
            pltpu.VMEM((PIECES, 4, 2, COLS, 128), bf), pltpu.VMEM((2, 4, 4, 2, COLS, 128), bf),
            pltpu.VMEM((4, 2, COLS, 128), bf), pltpu.VMEM((4, 2, COLS, 128), bf),
            pltpu.VMEM((PIECES, 3, 2, COLS, 128), bf),
            dma((2, PIECES)), dma((2, PIECES)), dma((2,)), dma((2,)), dma((PIECES,)), dma((2, 4)),
            dma, dma, dma((PIECES,)), dma((PIECES,)),
        ],
        compiler_params=pltpu.CompilerParams(collective_id=0, has_side_effects=True, vmem_limit_bytes=40 << 20),
    )(friction, dep, flags)


def per_device(particle_mass, particle_velocity, spline_weights, particle_cells, block_counts, friction, contact_flags):
    dep = deposit((8, 2, 0), block_counts.reshape(32), particle_mass, particle_velocity, spline_weights, particle_cells)
    return exchange(friction, dep, contact_flags)


def solution(mesh):
    return jax.shard_map(
        per_device,
        mesh=mesh,
        in_specs=(
            P("mat", "gz"),
            P("mat", None, "gz"),
            P("mat", None, "gz"),
            P("mat", "gz"),
            P("mat", "gz", None),
            P("mat"),
            P("gz", None, None),
        ),
        out_specs=P("mat", None, "gz", None, None),
        check_vma=False,
    )
```

```python
import functools
import jax
import jax.numpy as jnp
from jax import lax
from jax.experimental import pallas as pl
from jax.experimental.pallas import tpu as pltpu
from jax.sharding import PartitionSpec as P

BLOCKS = 32
SLOTS = 4096
ROWS = SLOTS // 128
UR = 4
UNIT = UR * 128
PER_BLOCK = SLOTS // UNIT
W = 24
HEAD = 4
F32, BF = jnp.float32, jnp.bfloat16


def deposit_kernel(U, XP, ORDER, counts, mass_h, vel_h, wt_h, cells_h, out, mass, vel, wt, cells, acc, tbuf, prep,
                   lbuf, rbuf, obuf, urow, uleft, ubase, in_sem, out_sem):
    chunks = U * UR // 2

    def copies(q):
        first, count = ((0, HEAD), (HEAD, BLOCKS - HEAD))[q]
        r = pl.ds(first * ROWS, count * ROWS)
        return [pltpu.make_async_copy(mass_h.at[r], mass.at[r], in_sem.at[0, q]),
                pltpu.make_async_copy(vel_h.at[:, r], vel.at[:, r], in_sem.at[1, q]),
                pltpu.make_async_copy(wt_h.at[:, r], wt.at[:, r], in_sem.at[2, q]),
                pltpu.make_async_copy(cells_h.at[r], cells.at[r], in_sem.at[3, q])]

    for q in range(2):
        for c in copies(q):
            c.start()

    sub = lax.broadcasted_iota(jnp.int32, (8, 128), 0)
    usub = lax.broadcasted_iota(jnp.int32, (UR, 128), 0)
    place_id = usub * 128 + lax.broadcasted_iota(jnp.int32, (UR, 128), 1)
    odd = (usub & 1) == 1
    row16 = lax.broadcasted_iota(jnp.int32, (16, 128), 0)

    def const(values):
        return values.astype(F32).astype(BF)

    xcon = [const((row16 - p + 1) & 15) for p in range(3)]
    ycon = [const(row16 - t) for t in range(3)]
    ycon_b = [const(16 + (row16 & 7) - t) for t in range(3)]
    upper = const(row16) < jnp.asarray(8, BF)
    zero = jnp.zeros((), BF)
    one = jnp.ones((), BF)

    def dead(i, row):
        urow[i] = row
        uleft[i] = 0

    for i in range(2 * U):
        dead(i, 0)
    for i in range(2 * chunks):
        ubase[i] = 0

    def list_block(b, at):
        n = counts[b]
        for c in range(PER_BLOCK):
            urow[at + c] = b * ROWS + c * UR
            uleft[at + c] = n - c * UNIT
        return at + (n + (UNIT - 1)) // UNIT

    head_end = lax.fori_loop(0, HEAD, list_block, 2 * U)
    end = lax.fori_loop(HEAD, BLOCKS, list_block, head_end)
    for i in range(3 * U):
        dead(end + i, BLOCKS * ROWS - UR)

    def clear(b, _):
        acc[b] = jnp.zeros(acc.shape[1:], F32)
        return 0

    lax.fori_loop(0, BLOCKS, clear, 0)
    prep[...] = jnp.zeros(prep.shape, F32)
    lbuf[...] = jnp.zeros(lbuf.shape, BF)
    rbuf[...] = jnp.zeros(rbuf.shape, BF)

    def prepare(slot, unit):
        row = urow[unit]
        rr = pl.ds(pl.multiple_of(row, UR), UR)
        cl = cells[rr, :]
        live = place_id < uleft[unit]
        m = jnp.where(live, mass[rr, :], 0.0)
        y = cl & 127
        first = jnp.broadcast_to(y[:, 0:1], (UR, 128)) & ~7
        before = jnp.concatenate([first[0:1]] + [first[i - 1:i] for i in range(1, UR)], 0)
        first = jnp.where(odd, before, first)
        yrel = y - first
        top = cl >= 1024
        w = [wt[a, rr, :] for a in range(3)]
        prep[slot, 0] = yrel.astype(F32)
        prep[slot, 1] = ((cl >> 7) & 7).astype(F32)
        w = [m * v for v in w]
        prep[slot, 2] = jnp.where(top, 0.0, w[0])
        prep[slot, 3] = jnp.where(top, w[0], w[1])
        prep[slot, 4] = jnp.where(top, w[1], w[2])
        prep[slot, 5] = jnp.where(top, w[2], 0.0)
        return [first[2 * j, 0] for j in range(UR // 2)], jnp.where(live, yrel, 0)

    def build(i, slot, unit, j):
        row = urow[unit]
        for k in range(2):
            r = 2 * j + k

            def wide(tile):
                return jnp.broadcast_to(tile, (16, 128)).astype(BF)

            def own(q):
                return wide(prep[slot, q, r:r + 1, :])

            def weight(q):
                return wide(wt[q, pl.ds(row + r, 1), :])

            def taps(index, con, w):
                tile = jnp.where(index == con[0], w[0], zero)
                tile = jnp.where(index == con[1], w[1], tile)
                return jnp.where(index == con[2], w[2], tile)

            lanes = slice(k * 128, (k + 1) * 128)
            xw = taps(own(1), xcon, [weight(3 + p) for p in range(3)])
            for z in range(4):
                lbuf[i, z * 16:(z + 1) * 16, lanes] = own(2 + z) * xw
            wy = [weight(6 + t) for t in range(3)]
            yb = own(0)
            ya, yz = taps(yb, ycon, wy), taps(yb, ycon_b, wy)
            v = [wide(vel[d, pl.ds(row + r, 1), :]) for d in range(3)]
            rbuf[i, 0:16, lanes] = ya
            for d in range(3):
                rbuf[i, (d + 1) * 16:(d + 2) * 16, lanes] = v[d] * ya
            rbuf[i, 64:80, lanes] = jnp.where(upper, one, v[0]) * yz
            rbuf[i, 80:96, lanes] = jnp.where(upper, v[1], v[2]) * yz

    def multiply(i, b, base):
        res = lax.dot_general(rbuf[i], lbuf[i], (((1,), (1,)), ((), ())), preferred_element_type=F32)
        for f in range(4):
            acc[b, f, pl.ds(pl.multiple_of(base, 8), 16), 0:64] += res[16 * f:16 * f + 16]
            acc[b, f, pl.ds(pl.multiple_of(base + 16, 8), 8), 0:64] += res[64 + 8 * f:72 + 8 * f]

    def turn(b):
        for h in range(2):
            def rows(f):
                head = acc[b, f, 1:9] + jnp.where(sub == 0, acc[b, f, 129:137], 0.0)
                tail = acc[b, f, 121:129] + jnp.where(sub == 7, jnp.broadcast_to(acc[b, f, 0:1], (8, 128)), 0.0)
                return jnp.concatenate([head, acc[b, f, 9:121], tail], 0)
            tbuf[b, h] = (rows(2 * h) + pltpu.roll(rows(2 * h + 1), 64, 1)).T

    def group(g, state):
        t, far_before = state
        at = g * U
        more = jnp.max(far_before) >= W - 2
        far = None
        if XP and ORDER == 0:
            for k in range(XP):
                turn(jnp.minimum(t + k, BLOCKS - 1))
        for k in range(U):
            if XP and ORDER == 1 and k % (U // XP) == 0:
                turn(jnp.minimum(t + k // (U // XP), BLOCKS - 1))
            for j in range(UR // 2):
                i = k * (UR // 2) + j
                multiply(i, urow[at + k] // ROWS, ubase[2 * at + i])
                build(i, k, at + U + k, j)
            bases, spread = prepare(k, at + 2 * U + k)
            for j in range(UR // 2):
                ubase[2 * (at + 2 * U) + k * (UR // 2) + j] = bases[j]
            far = spread if far is None else jnp.maximum(far, spread)

        if XP:
            t = jnp.maximum(t, jnp.minimum(t + XP, urow[at] // ROWS))

        @pl.when(more)
        def _():
            def again(k, _):
                unit = at + U + k
                b = urow[unit] // ROWS
                prepare(U, unit)

                def window(off, _):
                    prep[U, 0] = prep[U, 0] - float(W)
                    for j in range(UR // 2):
                        base = ubase[2 * unit + j] + off * W

                        @pl.when(base < 130)
                        def _():
                            build(chunks, U, unit, j)
                            multiply(chunks, b, base)
                    return 0

                lax.fori_loop(1, 6, window, 0)
                return 0

            lax.fori_loop(0, U, again, 0)

        return t, far

    for c in copies(0):
        c.wait()
    head_groups = (head_end - 2 * U) // U
    state = lax.fori_loop(0, head_groups, group, (0, jnp.zeros((UR, 128), jnp.int32)))
    for c in copies(1):
        c.wait()
    t, _ = lax.fori_loop(head_groups, (end + U - 1) // U, group, state)

    def rest(k, _):
        for j in range(4):
            turn(jnp.minimum(t + 4 * k + j, BLOCKS - 1))
        return 0

    lax.fori_loop(0, (BLOCKS - t + 3) // 4, rest, 0)

    def piece(p):
        return pltpu.make_async_copy(obuf.at[p], out.at[p], out_sem.at[p])

    def seams(p, _):
        for j in range(4):
            b = p * 4 + j
            dn = (b + BLOCKS - 1) & (BLOCKS - 1)
            up = (b + 1) & (BLOCKS - 1)
            for k in range(16):
                o = (k // 4 % 2) * 64 + k % 4 * 16
                h = k // 8
                obuf[p, k, 8 * j:8 * j + 8, :] = (
                    tbuf[b, h, o:o + 8]
                    + jnp.where(sub == 0, tbuf[dn, h, o + 8:o + 16], 0.0)
                    + jnp.where(sub == 7, tbuf[up, h, o + 8:o + 16], 0.0))
        piece(p).start()
        return 0

    lax.fori_loop(0, 8, seams, 0)

    def drain_out(p, _):
        piece(p).wait()
        return 0

    lax.fori_loop(0, 8, drain_out, 0)


def deposit(cfg, counts, mass, vel, wt, cells):
    U, XP, ORDER = cfg
    chunks = U * UR // 2
    hbm = pl.BlockSpec(memory_space=pltpu.MemorySpace.HBM)
    units = BLOCKS * PER_BLOCK + 5 * U + PER_BLOCK
    return pl.pallas_call(
        functools.partial(deposit_kernel, U, XP, ORDER),
        in_specs=[pl.BlockSpec(memory_space=pltpu.SMEM), hbm, hbm, hbm, hbm],
        out_specs=hbm,
        out_shape=jax.ShapeDtypeStruct((112, 16, 32, 128), F32),
        scratch_shapes=[
            pltpu.VMEM((1024, 128), F32), pltpu.VMEM((3, 1024, 128), F32), pltpu.VMEM((9, 1024, 128), F32),
            pltpu.VMEM((1024, 128), jnp.int32), pltpu.VMEM((BLOCKS, 4, 160, 128), F32),
            pltpu.VMEM((BLOCKS, 2, 128, 128), F32), pltpu.VMEM((U + 1, 6, UR, 128), F32),
            pltpu.VMEM((chunks + 1, 64, 256), BF), pltpu.VMEM((chunks + 1, 4 * W, 256), BF),
            pltpu.VMEM((8, 16, 32, 128), F32),
            pltpu.SMEM((units,), jnp.int32), pltpu.SMEM((units,), jnp.int32), pltpu.SMEM((2 * units,), jnp.int32),
            pltpu.SemaphoreType.DMA((4, 2)), pltpu.SemaphoreType.DMA((8,)),
        ],
        compiler_params=pltpu.CompilerParams(vmem_limit_bytes=60 << 20),
    )(counts, mass.reshape(1024, 128), vel.reshape(3, 1024, 128), wt.reshape(9, 1024, 128), cells.reshape(1024, 128))


MASS_FLOOR = 0.2
GRADIENT_FLOOR = 0.1
SLIP_FLOOR = 0.05
PIECES = 8
COLS = 32
MID = 7
MESH = pl.DeviceIdType.MESH


def comm_kernel(fric, dep_h, flags_h, out, dep, flags, d_s, f_s, hsend, hrecv, msend, mrecv, nf, mass, rsend, rrecv, ysend,
                yrecv, cbuf, h_ss, h_rs, m_ss, m_rs, r_ss, r_rs, y_ss, y_rs, c_ss, c_rs):
    slabs = lax.axis_size("gz")
    g = lax.axis_index("gz")
    me = lax.axis_index("mat")
    lo = lax.rem(g + slabs - 1, slabs)
    hi = lax.rem(g + 1, slabs)
    s_lo = jnp.where(g == 0, 0.0, 1.0)
    s_hi = jnp.where(g == slabs - 1, 0.0, 1.0)

    def fetch(p):
        return pltpu.make_async_copy(dep_h.at[p], dep.at[p], d_s.at[p])

    def start_fetch(k, _):
        fetch(lax.rem(me + 1 + k, PIECES)).start()
        return 0

    lax.fori_loop(0, PIECES, start_fetch, 0)
    fetch_flags = pltpu.make_async_copy(flags_h, flags, f_s)
    fetch_flags.start()

    barrier = pltpu.get_barrier_semaphore()
    for other in (lo, hi):
        pl.semaphore_signal(barrier, inc=1, device_id={"gz": other, "mat": me}, device_id_type=MESH)
    for k in range(1, PIECES):
        pl.semaphore_signal(barrier, inc=1, device_id={"gz": g, "mat": lax.rem(me + k, PIECES)},
                            device_id_type=MESH)

    def halo(side, p):
        return pltpu.make_async_remote_copy(
            src_ref=hsend.at[side, p], dst_ref=hrecv.at[side, p],
            send_sem=h_ss.at[side, p], recv_sem=h_rs.at[side, p],
            device_id={"gz": lo if side == 0 else hi, "mat": me}, device_id_type=MESH)

    x_me = me // 2
    y_me = me % 2

    def order(k):
        return lax.rem(x_me + 1 + k, 4) * 2 + jnp.where(k < 4, 1 - y_me, y_me)

    def edge(side):
        return pltpu.make_async_remote_copy(
            src_ref=msend.at[side], dst_ref=mrecv.at[side], send_sem=m_ss.at[side], recv_sem=m_rs.at[side],
            device_id={"gz": lo if side == 0 else hi, "mat": me}, device_id_type=MESH)

    def share(k):
        half = k // 4
        return pltpu.make_async_remote_copy(
            src_ref=rsend.at[order(k)], dst_ref=rrecv.at[half, x_me], send_sem=r_ss.at[k],
            recv_sem=r_rs.at[half, x_me],
            device_id={"gz": g, "mat": lax.rem(x_me + 1 + k, 4) * 2 + y_me}, device_id_type=MESH)

    def shared(half, x):
        return pltpu.make_async_remote_copy(
            src_ref=rsend.at[0], dst_ref=rrecv.at[half, x], send_sem=r_ss.at[0], recv_sem=r_rs.at[half, x],
            device_id={"gz": g, "mat": x * 2 + y_me}, device_id_type=MESH)

    def cross():
        return pltpu.make_async_remote_copy(
            src_ref=ysend, dst_ref=yrecv, send_sem=y_ss, recv_sem=y_rs,
            device_id={"gz": g, "mat": x_me * 2 + 1 - y_me}, device_id_type=MESH)

    def spread(p):
        return pltpu.make_async_remote_copy(
            src_ref=cbuf.at[me], dst_ref=cbuf.at[me], send_sem=c_ss.at[p], recv_sem=c_rs.at[me],
            device_id={"gz": g, "mat": p}, device_id_type=MESH)

    def spreaded(p):
        return pltpu.make_async_remote_copy(
            src_ref=cbuf.at[p], dst_ref=cbuf.at[p], send_sem=c_ss.at[p], recv_sem=c_rs.at[p],
            device_id={"gz": g, "mat": p}, device_id_type=MESH)

    def cols(p):
        return pl.ds(pl.multiple_of(p * COLS, COLS), COLS)

    def pack(k, _):
        p = order(k)
        fetch(p).wait()
        for f in range(4):
            hsend[0, p, f] = dep[p, 4 * f + 0].astype(jnp.bfloat16)
            hsend[1, p, f] = dep[p, 4 * f + 3].astype(jnp.bfloat16)
        msend[0, cols(p), :] = dep[p, 1].astype(jnp.bfloat16)
        msend[1, cols(p), :] = dep[p, 2].astype(jnp.bfloat16)
        return 0

    lax.fori_loop(0, PIECES, pack, 0)
    pl.semaphore_wait(barrier, PIECES + 1)

    def start_halo(k, _):
        p = order(k)
        halo(0, p).start()
        halo(1, p).start()
        return 0

    lax.fori_loop(0, PIECES, start_halo, 0)

    def nodes(p):
        halo(0, p).wait_recv()
        halo(1, p).wait_recv()
        x = cols(p)
        for f in range(4):
            low = dep[p, 4 * f + 1] + s_lo * hrecv[1, p, f].astype(jnp.float32)
            high = dep[p, 4 * f + 2] + s_hi * hrecv[0, p, f].astype(jnp.float32)
            nf[f, 0, x, :] = low
            nf[f, 1, x, :] = high
            rsend[p, f, 0] = low.astype(jnp.bfloat16)
            rsend[p, f, 1] = high.astype(jnp.bfloat16)
            if f == 0:
                xm = pl.ds(pl.multiple_of(p * COLS + 8, 8), COLS)
                mass[0, xm, :] = low
                mass[1, xm, :] = high

    def reduce_step(k, _):
        nodes(order(k))
        share(k).start()
        return 0

    def total_step(half):
        def step(k, total):
            x = lax.rem(x_me + 3 - k, 4)
            shared(half, x).wait_recv()
            return total + rrecv[half, x].astype(jnp.float32)
        own = rsend[order(4 * half + 3)].astype(jnp.float32)
        return lax.fori_loop(0, 3, step, own)

    lax.fori_loop(0, 3, reduce_step, 0)
    nodes(order(3))
    lax.fori_loop(4, MID, reduce_step, 0)
    ysend[...] = total_step(0).astype(jnp.bfloat16)
    cross().start()
    edge(0).start()
    edge(1).start()
    lax.fori_loop(MID, 7, reduce_step, 0)
    nodes(me)
    for z in range(2):
        mass[z, 7:8, :] = mass[z, 263:264, :]
        mass[z, 264:265, :] = mass[z, 8:9, :]

    total = total_step(1)
    cross().wait_recv()
    total = total + yrecv[...].astype(jnp.float32)
    cbuf[me] = (total[1:] / jnp.maximum(total[0], MASS_FLOOR)).astype(jnp.bfloat16)

    def start_spread(k, _):
        spread(lax.rem(me + 1 + k, PIECES)).start()
        return 0

    lax.fori_loop(0, PIECES - 1, start_spread, 0)
    friction = fric[0]
    fetch_flags.wait()
    edge(0).wait_recv()
    edge(1).wait_recv()

    def finish(p):
        for z in range(2):
            x = cols(p)
            m = nf[0, z, x, :]
            gx = mass[z, pl.ds(p * COLS + 9, COLS), :] - mass[z, pl.ds(p * COLS + 7, COLS), :]
            gy = pltpu.roll(m, 127, 1) - pltpu.roll(m, 1, 1)
            if z == 0:
                below = s_lo * (mrecv[1, x, :].astype(jnp.float32) + dep[p, 0])
                gz = nf[0, 1, x, :] - below
            else:
                above = s_hi * (mrecv[0, x, :].astype(jnp.float32) + dep[p, 3])
                gz = above - nf[0, 0, x, :]
            inv = lax.rsqrt(jnp.maximum(gz * gz + gx * gx + gy * gy, 4.0 * GRADIENT_FLOOR * GRADIENT_FLOOR))
            normal = [gz * inv, gx * inv, gy * inv]
            inv_m = 1.0 / jnp.maximum(m, MASS_FLOOR)
            speed = [nf[1 + d, z, x, :] * inv_m for d in range(3)]
            rel = [speed[d] - cbuf[p, d, z].astype(jnp.float32) for d in range(3)]
            part = rel[0] * normal[0] + rel[1] * normal[1] + rel[2] * normal[2]
            approach = jnp.maximum(part, 0.0)
            tangent = [rel[d] - part * normal[d] for d in range(3)]
            slip2 = tangent[0] * tangent[0] + tangent[1] * tangent[1] + tangent[2] * tangent[2]
            slip = slip2 * lax.rsqrt(jnp.maximum(slip2, 1.2e-38))
            factor = jnp.minimum(friction * approach, slip) * lax.rsqrt(jnp.maximum(slip2, SLIP_FLOOR * SLIP_FLOOR))
            flag = flags[z, x, :].astype(jnp.float32)
            for d in range(3):
                out[0, d, z, x, :] = speed[d] - flag * (approach * normal[d] + factor * tangent[d])

    finish(me)
    def finish_step(k, _):
        p = lax.rem(me + PIECES - 1 - k, PIECES)
        spreaded(p).wait_recv()
        finish(p)
        return 0

    lax.fori_loop(0, PIECES - 1, finish_step, 0)

    def drain(k, _):
        p = lax.rem(me + 1 + k, PIECES)
        spread(p).wait_send()
        return 0

    lax.fori_loop(0, PIECES - 1, drain, 0)

    def drain_share(k, _):
        share(k).wait_send()
        share(k + 4).wait_send()
        return 0

    lax.fori_loop(0, 3, drain_share, 0)
    cross().wait_send()
    edge(0).wait_send()
    edge(1).wait_send()

    def drain_halo(p, _):
        halo(0, p).wait_send()
        halo(1, p).wait_send()
        return 0

    lax.fori_loop(0, PIECES, drain_halo, 0)


def exchange(friction, dep, flags):
    hbm = pl.BlockSpec(memory_space=pltpu.MemorySpace.HBM)
    f32, bf = jnp.float32, jnp.bfloat16
    dma = pltpu.SemaphoreType.DMA
    return pl.pallas_call(
        comm_kernel,
        in_specs=[pl.BlockSpec(memory_space=pltpu.SMEM), hbm, hbm],
        out_specs=pl.BlockSpec(memory_space=pltpu.VMEM),
        out_shape=jax.ShapeDtypeStruct((1, 3, 2, 256, 128), f32),
        scratch_shapes=[
            pltpu.VMEM((PIECES, 16, COLS, 128), f32), pltpu.VMEM((2, 256, 128), jnp.int32),
            dma((PIECES,)), dma,
            pltpu.VMEM((2, PIECES, 4, COLS, 128), bf), pltpu.VMEM((2, PIECES, 4, COLS, 128), bf),
            pltpu.VMEM((2, 256, 128), bf), pltpu.VMEM((2, 256, 128), bf),
            pltpu.VMEM((4, 2, 256, 128), f32), pltpu.VMEM((2, 272, 128), f32),
            pltpu.VMEM((PIECES, 4, 2, COLS, 128), bf), pltpu.VMEM((2, 4, 4, 2, COLS, 128), bf),
            pltpu.VMEM((4, 2, COLS, 128), bf), pltpu.VMEM((4, 2, COLS, 128), bf),
            pltpu.VMEM((PIECES, 3, 2, COLS, 128), bf),
            dma((2, PIECES)), dma((2, PIECES)), dma((2,)), dma((2,)), dma((PIECES,)), dma((2, 4)),
            dma, dma, dma((PIECES,)), dma((PIECES,)),
        ],
        compiler_params=pltpu.CompilerParams(collective_id=0, has_side_effects=True, vmem_limit_bytes=40 << 20),
    )(friction, dep, flags)


def per_device(particle_mass, particle_velocity, spline_weights, particle_cells, block_counts, friction, contact_flags):
    dep = deposit((8, 2, 0), block_counts.reshape(32), particle_mass, particle_velocity, spline_weights, particle_cells)
    return exchange(friction, dep, contact_flags)


def solution(mesh):
    return jax.shard_map(
        per_device,
        mesh=mesh,
        in_specs=(
            P("mat", "gz"),
            P("mat", None, "gz"),
            P("mat", None, "gz"),
            P("mat", "gz"),
            P("mat", "gz", None),
            P("mat"),
            P("gz", None, None),
        ),
        out_specs=P("mat", None, "gz", None, None),
        check_vma=False,
    )
```

```python
import functools
import jax
import jax.numpy as jnp
from jax import lax
from jax.experimental import pallas as pl
from jax.experimental.pallas import tpu as pltpu
from jax.sharding import PartitionSpec as P

BLOCKS = 32
SLOTS = 4096
ROWS = SLOTS // 128
UR = 4
UNIT = UR * 128
PER_BLOCK = SLOTS // UNIT
W = 24
HEAD = 6
F32, BF = jnp.float32, jnp.bfloat16


def deposit_kernel(U, XP, ORDER, counts, mass_h, vel_h, wt_h, cells_h, out, mass, vel, wt, cells, acc, tbuf, prep,
                   lbuf, rbuf, obuf, urow, uleft, ubase, in_sem, out_sem):
    chunks = U * UR // 2

    def copies(q):
        first, count = ((0, HEAD), (HEAD, BLOCKS - HEAD))[q]
        r = pl.ds(first * ROWS, count * ROWS)
        return [pltpu.make_async_copy(mass_h.at[r], mass.at[r], in_sem.at[0, q]),
                pltpu.make_async_copy(vel_h.at[:, r], vel.at[:, r], in_sem.at[1, q]),
                pltpu.make_async_copy(wt_h.at[:, r], wt.at[:, r], in_sem.at[2, q]),
                pltpu.make_async_copy(cells_h.at[r], cells.at[r], in_sem.at[3, q])]

    for q in range(2):
        for c in copies(q):
            c.start()

    sub = lax.broadcasted_iota(jnp.int32, (8, 128), 0)
    usub = lax.broadcasted_iota(jnp.int32, (UR, 128), 0)
    place_id = usub * 128 + lax.broadcasted_iota(jnp.int32, (UR, 128), 1)
    odd = (usub & 1) == 1
    row16 = lax.broadcasted_iota(jnp.int32, (16, 128), 0)

    def const(values):
        return values.astype(F32).astype(BF)

    xcon = [const((row16 - p + 1) & 15) for p in range(3)]
    ycon = [const(row16 - t) for t in range(3)]
    ycon_b = [const(16 + (row16 & 7) - t) for t in range(3)]
    upper = const(row16) < jnp.asarray(8, BF)
    zero = jnp.zeros((), BF)
    one = jnp.ones((), BF)

    def dead(i, row):
        urow[i] = row
        uleft[i] = 0

    for i in range(2 * U):
        dead(i, 0)
    for i in range(2 * chunks):
        ubase[i] = 0

    def list_block(b, at):
        n = counts[b]
        for c in range(PER_BLOCK):
            urow[at + c] = b * ROWS + c * UR
            uleft[at + c] = n - c * UNIT
        acc[b] = jnp.zeros(acc.shape[1:], F32)
        return at + (n + (UNIT - 1)) // UNIT

    prep[...] = jnp.zeros(prep.shape, F32)
    lbuf[...] = jnp.zeros(lbuf.shape, BF)
    rbuf[...] = jnp.zeros(rbuf.shape, BF)
    head_end = lax.fori_loop(0, HEAD, list_block, 2 * U)
    end = lax.fori_loop(HEAD, BLOCKS, list_block, head_end)
    for i in range(3 * U):
        dead(end + i, BLOCKS * ROWS - UR)


    def prepare(slot, unit):
        row = urow[unit]
        rr = pl.ds(pl.multiple_of(row, UR), UR)
        cl = cells[rr, :]
        live = place_id < uleft[unit]
        m = jnp.where(live, mass[rr, :], 0.0)
        y = cl & 127
        first = jnp.broadcast_to(y[:, 0:1], (UR, 128)) & ~7
        before = jnp.concatenate([first[0:1]] + [first[i - 1:i] for i in range(1, UR)], 0)
        first = jnp.where(odd, before, first)
        yrel = y - first
        top = cl >= 1024
        w = [wt[a, rr, :] for a in range(3)]
        prep[slot, 0] = yrel.astype(F32)
        prep[slot, 1] = ((cl >> 7) & 7).astype(F32)
        w = [m * v for v in w]
        prep[slot, 2] = jnp.where(top, 0.0, w[0])
        prep[slot, 3] = jnp.where(top, w[0], w[1])
        prep[slot, 4] = jnp.where(top, w[1], w[2])
        prep[slot, 5] = jnp.where(top, w[2], 0.0)
        return [first[2 * j, 0] for j in range(UR // 2)], jnp.where(live, yrel, 0)

    def build(i, slot, unit, j):
        row = urow[unit]
        for k in range(2):
            r = 2 * j + k

            def wide(tile):
                return jnp.broadcast_to(tile, (16, 128)).astype(BF)

            def own(q):
                return wide(prep[slot, q, r:r + 1, :])

            def weight(q):
                return wide(wt[q, pl.ds(row + r, 1), :])

            def taps(index, con, w):
                tile = jnp.where(index == con[0], w[0], zero)
                tile = jnp.where(index == con[1], w[1], tile)
                return jnp.where(index == con[2], w[2], tile)

            lanes = slice(k * 128, (k + 1) * 128)
            xw = taps(own(1), xcon, [weight(3 + p) for p in range(3)])
            for z in range(4):
                lbuf[i, z * 16:(z + 1) * 16, lanes] = own(2 + z) * xw
            wy = [weight(6 + t) for t in range(3)]
            yb = own(0)
            ya, yz = taps(yb, ycon, wy), taps(yb, ycon_b, wy)
            v = [wide(vel[d, pl.ds(row + r, 1), :]) for d in range(3)]
            rbuf[i, 0:16, lanes] = ya
            for d in range(3):
                rbuf[i, (d + 1) * 16:(d + 2) * 16, lanes] = v[d] * ya
            rbuf[i, 64:80, lanes] = jnp.where(upper, one, v[0]) * yz
            rbuf[i, 80:96, lanes] = jnp.where(upper, v[1], v[2]) * yz

    def multiply(i, b, base):
        res = lax.dot_general(rbuf[i], lbuf[i], (((1,), (1,)), ((), ())), preferred_element_type=F32)
        for f in range(4):
            acc[b, f, pl.ds(pl.multiple_of(base, 8), 16), 0:64] += res[16 * f:16 * f + 16]
            acc[b, f, pl.ds(pl.multiple_of(base + 16, 8), 8), 0:64] += res[64 + 8 * f:72 + 8 * f]

    def turn(b):
        for h in range(2):
            def rows(f):
                head = acc[b, f, 1:9] + jnp.where(sub == 0, acc[b, f, 129:137], 0.0)
                tail = acc[b, f, 121:129] + jnp.where(sub == 7, jnp.broadcast_to(acc[b, f, 0:1], (8, 128)), 0.0)
                return jnp.concatenate([head, acc[b, f, 9:121], tail], 0)
            tbuf[b, h] = (rows(2 * h) + pltpu.roll(rows(2 * h + 1), 64, 1)).T

    def group(g, state):
        t, far_before = state
        at = g * U
        more = jnp.max(far_before) >= W - 2
        far = None
        if XP and ORDER == 0:
            for k in range(XP):
                turn(jnp.minimum(t + k, BLOCKS - 1))
        for k in range(U):
            if XP and ORDER == 1 and k % (U // XP) == 0:
                turn(jnp.minimum(t + k // (U // XP), BLOCKS - 1))
            for j in range(UR // 2):
                i = k * (UR // 2) + j
                multiply(i, urow[at + k] // ROWS, ubase[2 * at + i])
                build(i, k, at + U + k, j)
            bases, spread = prepare(k, at + 2 * U + k)
            for j in range(UR // 2):
                ubase[2 * (at + 2 * U) + k * (UR // 2) + j] = bases[j]
            far = spread if far is None else jnp.maximum(far, spread)

        if XP:
            t = jnp.maximum(t, jnp.minimum(t + XP, urow[at] // ROWS))

        @pl.when(more)
        def _():
            def again(k, _):
                unit = at + U + k
                b = urow[unit] // ROWS
                prepare(U, unit)

                def window(off, _):
                    prep[U, 0] = prep[U, 0] - float(W)
                    for j in range(UR // 2):
                        base = ubase[2 * unit + j] + off * W

                        @pl.when(base < 130)
                        def _():
                            build(chunks, U, unit, j)
                            multiply(chunks, b, base)
                    return 0

                lax.fori_loop(1, 6, window, 0)
                return 0

            lax.fori_loop(0, U, again, 0)

        return t, far

    for c in copies(0):
        c.wait()
    head_groups = (head_end - 2 * U) // U
    state = lax.fori_loop(0, head_groups, group, (0, jnp.zeros((UR, 128), jnp.int32)))
    for c in copies(1):
        c.wait()
    t, _ = lax.fori_loop(head_groups, (end + U - 1) // U, group, state)

    def rest(k, _):
        for j in range(4):
            turn(jnp.minimum(t + 4 * k + j, BLOCKS - 1))
        return 0

    lax.fori_loop(0, (BLOCKS - t + 3) // 4, rest, 0)

    def piece(p):
        return pltpu.make_async_copy(obuf.at[p], out.at[p], out_sem.at[p])

    def seams(p, _):
        for j in range(4):
            b = p * 4 + j
            dn = (b + BLOCKS - 1) & (BLOCKS - 1)
            up = (b + 1) & (BLOCKS - 1)
            for k in range(16):
                o = (k // 4 % 2) * 64 + k % 4 * 16
                h = k // 8
                obuf[p, k, 8 * j:8 * j + 8, :] = (
                    tbuf[b, h, o:o + 8]
                    + jnp.where(sub == 0, tbuf[dn, h, o + 8:o + 16], 0.0)
                    + jnp.where(sub == 7, tbuf[up, h, o + 8:o + 16], 0.0))
        piece(p).start()
        return 0

    lax.fori_loop(0, 8, seams, 0)

    def drain_out(p, _):
        piece(p).wait()
        return 0

    lax.fori_loop(0, 8, drain_out, 0)


def deposit(cfg, counts, mass, vel, wt, cells):
    U, XP, ORDER = cfg
    chunks = U * UR // 2
    hbm = pl.BlockSpec(memory_space=pltpu.MemorySpace.HBM)
    units = BLOCKS * PER_BLOCK + 5 * U + PER_BLOCK
    return pl.pallas_call(
        functools.partial(deposit_kernel, U, XP, ORDER),
        in_specs=[pl.BlockSpec(memory_space=pltpu.SMEM), hbm, hbm, hbm, hbm],
        out_specs=hbm,
        out_shape=jax.ShapeDtypeStruct((112, 16, 32, 128), F32),
        scratch_shapes=[
            pltpu.VMEM((1024, 128), F32), pltpu.VMEM((3, 1024, 128), F32), pltpu.VMEM((9, 1024, 128), F32),
            pltpu.VMEM((1024, 128), jnp.int32), pltpu.VMEM((BLOCKS, 4, 152, 128), F32),
            pltpu.VMEM((BLOCKS, 2, 128, 128), F32), pltpu.VMEM((U + 1, 6, UR, 128), F32),
            pltpu.VMEM((chunks + 1, 64, 256), BF), pltpu.VMEM((chunks + 1, 4 * W, 256), BF),
            pltpu.VMEM((8, 16, 32, 128), F32),
            pltpu.SMEM((units,), jnp.int32), pltpu.SMEM((units,), jnp.int32), pltpu.SMEM((2 * units,), jnp.int32),
            pltpu.SemaphoreType.DMA((4, 2)), pltpu.SemaphoreType.DMA((8,)),
        ],
        compiler_params=pltpu.CompilerParams(vmem_limit_bytes=60 << 20),
    )(counts, mass.reshape(1024, 128), vel.reshape(3, 1024, 128), wt.reshape(9, 1024, 128), cells.reshape(1024, 128))


MASS_FLOOR = 0.2
GRADIENT_FLOOR = 0.1
SLIP_FLOOR = 0.05
PIECES = 8
COLS = 32
MID = 7
MESH = pl.DeviceIdType.MESH


def comm_kernel(fric, dep_h, flags_h, out, dep, flags, d_s, f_s, hsend, hrecv, msend, mrecv, nf, mass, rsend, rrecv, ysend,
                yrecv, cbuf, h_ss, h_rs, m_ss, m_rs, r_ss, r_rs, y_ss, y_rs, c_ss, c_rs):
    slabs = lax.axis_size("gz")
    g = lax.axis_index("gz")
    me = lax.axis_index("mat")
    lo = lax.rem(g + slabs - 1, slabs)
    hi = lax.rem(g + 1, slabs)
    s_lo = jnp.where(g == 0, 0.0, 1.0)
    s_hi = jnp.where(g == slabs - 1, 0.0, 1.0)

    def fetch(p):
        return pltpu.make_async_copy(dep_h.at[p], dep.at[p], d_s.at[p])

    def start_fetch(k, _):
        fetch(lax.rem(me + 1 + k, PIECES)).start()
        return 0

    lax.fori_loop(0, PIECES, start_fetch, 0)
    fetch_flags = pltpu.make_async_copy(flags_h, flags, f_s)
    fetch_flags.start()

    barrier = pltpu.get_barrier_semaphore()
    for other in (lo, hi):
        pl.semaphore_signal(barrier, inc=1, device_id={"gz": other, "mat": me}, device_id_type=MESH)
    for k in range(1, PIECES):
        pl.semaphore_signal(barrier, inc=1, device_id={"gz": g, "mat": lax.rem(me + k, PIECES)},
                            device_id_type=MESH)

    def halo(side, p):
        return pltpu.make_async_remote_copy(
            src_ref=hsend.at[side, p], dst_ref=hrecv.at[side, p],
            send_sem=h_ss.at[side, p], recv_sem=h_rs.at[side, p],
            device_id={"gz": lo if side == 0 else hi, "mat": me}, device_id_type=MESH)

    x_me = me // 2
    y_me = me % 2

    def order(k):
        return lax.rem(x_me + 1 + k, 4) * 2 + jnp.where(k < 4, 1 - y_me, y_me)

    def edge(side):
        return pltpu.make_async_remote_copy(
            src_ref=msend.at[side], dst_ref=mrecv.at[side], send_sem=m_ss.at[side], recv_sem=m_rs.at[side],
            device_id={"gz": lo if side == 0 else hi, "mat": me}, device_id_type=MESH)

    def share(k):
        half = k // 4
        return pltpu.make_async_remote_copy(
            src_ref=rsend.at[order(k)], dst_ref=rrecv.at[half, x_me], send_sem=r_ss.at[k],
            recv_sem=r_rs.at[half, x_me],
            device_id={"gz": g, "mat": lax.rem(x_me + 1 + k, 4) * 2 + y_me}, device_id_type=MESH)

    def shared(half, x):
        return pltpu.make_async_remote_copy(
            src_ref=rsend.at[0], dst_ref=rrecv.at[half, x], send_sem=r_ss.at[0], recv_sem=r_rs.at[half, x],
            device_id={"gz": g, "mat": x * 2 + y_me}, device_id_type=MESH)

    def cross():
        return pltpu.make_async_remote_copy(
            src_ref=ysend, dst_ref=yrecv, send_sem=y_ss, recv_sem=y_rs,
            device_id={"gz": g, "mat": x_me * 2 + 1 - y_me}, device_id_type=MESH)

    def spread(p):
        return pltpu.make_async_remote_copy(
            src_ref=cbuf.at[me], dst_ref=cbuf.at[me], send_sem=c_ss.at[p], recv_sem=c_rs.at[me],
            device_id={"gz": g, "mat": p}, device_id_type=MESH)

    def spreaded(p):
        return pltpu.make_async_remote_copy(
            src_ref=cbuf.at[p], dst_ref=cbuf.at[p], send_sem=c_ss.at[p], recv_sem=c_rs.at[p],
            device_id={"gz": g, "mat": p}, device_id_type=MESH)

    def cols(p):
        return pl.ds(pl.multiple_of(p * COLS, COLS), COLS)

    def pack(k, _):
        p = order(k)
        fetch(p).wait()
        for f in range(4):
            hsend[0, p, f] = dep[p, 4 * f + 0].astype(jnp.bfloat16)
            hsend[1, p, f] = dep[p, 4 * f + 3].astype(jnp.bfloat16)
        msend[0, cols(p), :] = dep[p, 1].astype(jnp.bfloat16)
        msend[1, cols(p), :] = dep[p, 2].astype(jnp.bfloat16)
        return 0

    lax.fori_loop(0, PIECES, pack, 0)
    pl.semaphore_wait(barrier, PIECES + 1)

    def start_halo(k, _):
        p = order(k)
        halo(0, p).start()
        halo(1, p).start()
        return 0

    lax.fori_loop(0, PIECES, start_halo, 0)

    def nodes(p):
        halo(0, p).wait_recv()
        halo(1, p).wait_recv()
        x = cols(p)
        for f in range(4):
            low = dep[p, 4 * f + 1] + s_lo * hrecv[1, p, f].astype(jnp.float32)
            high = dep[p, 4 * f + 2] + s_hi * hrecv[0, p, f].astype(jnp.float32)
            nf[f, 0, x, :] = low
            nf[f, 1, x, :] = high
            rsend[p, f, 0] = low.astype(jnp.bfloat16)
            rsend[p, f, 1] = high.astype(jnp.bfloat16)
            if f == 0:
                xm = pl.ds(pl.multiple_of(p * COLS + 8, 8), COLS)
                mass[0, xm, :] = low
                mass[1, xm, :] = high

    def reduce_step(k, _):
        nodes(order(k))
        share(k).start()
        return 0

    def total_step(half):
        def step(k, total):
            x = lax.rem(x_me + 3 - k, 4)
            shared(half, x).wait_recv()
            return total + rrecv[half, x].astype(jnp.float32)
        own = rsend[order(4 * half + 3)].astype(jnp.float32)
        return lax.fori_loop(0, 3, step, own)

    lax.fori_loop(0, 3, reduce_step, 0)
    nodes(order(3))
    lax.fori_loop(4, MID, reduce_step, 0)
    ysend[...] = total_step(0).astype(jnp.bfloat16)
    cross().start()
    edge(0).start()
    edge(1).start()
    lax.fori_loop(MID, 7, reduce_step, 0)
    nodes(me)
    for z in range(2):
        mass[z, 7:8, :] = mass[z, 263:264, :]
        mass[z, 264:265, :] = mass[z, 8:9, :]

    total = total_step(1)
    cross().wait_recv()
    total = total + yrecv[...].astype(jnp.float32)
    cbuf[me] = (total[1:] / jnp.maximum(total[0], MASS_FLOOR)).astype(jnp.bfloat16)

    def start_spread(k, _):
        spread(lax.rem(me + 1 + k, PIECES)).start()
        return 0

    lax.fori_loop(0, PIECES - 1, start_spread, 0)
    friction = fric[0]
    fetch_flags.wait()
    edge(0).wait_recv()
    edge(1).wait_recv()

    def finish(p):
        for z in range(2):
            x = cols(p)
            m = nf[0, z, x, :]
            gx = mass[z, pl.ds(p * COLS + 9, COLS), :] - mass[z, pl.ds(p * COLS + 7, COLS), :]
            gy = pltpu.roll(m, 127, 1) - pltpu.roll(m, 1, 1)
            if z == 0:
                below = s_lo * (mrecv[1, x, :].astype(jnp.float32) + dep[p, 0])
                gz = nf[0, 1, x, :] - below
            else:
                above = s_hi * (mrecv[0, x, :].astype(jnp.float32) + dep[p, 3])
                gz = above - nf[0, 0, x, :]
            inv = lax.rsqrt(jnp.maximum(gz * gz + gx * gx + gy * gy, 4.0 * GRADIENT_FLOOR * GRADIENT_FLOOR))
            normal = [gz * inv, gx * inv, gy * inv]
            inv_m = 1.0 / jnp.maximum(m, MASS_FLOOR)
            speed = [nf[1 + d, z, x, :] * inv_m for d in range(3)]
            rel = [speed[d] - cbuf[p, d, z].astype(jnp.float32) for d in range(3)]
            part = rel[0] * normal[0] + rel[1] * normal[1] + rel[2] * normal[2]
            approach = jnp.maximum(part, 0.0)
            tangent = [rel[d] - part * normal[d] for d in range(3)]
            slip2 = tangent[0] * tangent[0] + tangent[1] * tangent[1] + tangent[2] * tangent[2]
            slip = slip2 * lax.rsqrt(jnp.maximum(slip2, 1.2e-38))
            factor = jnp.minimum(friction * approach, slip) * lax.rsqrt(jnp.maximum(slip2, SLIP_FLOOR * SLIP_FLOOR))
            flag = flags[z, x, :].astype(jnp.float32)
            for d in range(3):
                out[0, d, z, x, :] = speed[d] - flag * (approach * normal[d] + factor * tangent[d])

    finish(me)
    def finish_step(k, _):
        p = lax.rem(me + PIECES - 1 - k, PIECES)
        spreaded(p).wait_recv()
        finish(p)
        return 0

    lax.fori_loop(0, PIECES - 1, finish_step, 0)

    def drain(k, _):
        p = lax.rem(me + 1 + k, PIECES)
        spread(p).wait_send()
        return 0

    lax.fori_loop(0, PIECES - 1, drain, 0)

    def drain_share(k, _):
        share(k).wait_send()
        share(k + 4).wait_send()
        return 0

    lax.fori_loop(0, 3, drain_share, 0)
    cross().wait_send()
    edge(0).wait_send()
    edge(1).wait_send()

    def drain_halo(p, _):
        halo(0, p).wait_send()
        halo(1, p).wait_send()
        return 0

    lax.fori_loop(0, PIECES, drain_halo, 0)


def exchange(friction, dep, flags):
    hbm = pl.BlockSpec(memory_space=pltpu.MemorySpace.HBM)
    f32, bf = jnp.float32, jnp.bfloat16
    dma = pltpu.SemaphoreType.DMA
    return pl.pallas_call(
        comm_kernel,
        in_specs=[pl.BlockSpec(memory_space=pltpu.SMEM), hbm, hbm],
        out_specs=pl.BlockSpec(memory_space=pltpu.VMEM),
        out_shape=jax.ShapeDtypeStruct((1, 3, 2, 256, 128), f32),
        scratch_shapes=[
            pltpu.VMEM((PIECES, 16, COLS, 128), f32), pltpu.VMEM((2, 256, 128), jnp.int32),
            dma((PIECES,)), dma,
            pltpu.VMEM((2, PIECES, 4, COLS, 128), bf), pltpu.VMEM((2, PIECES, 4, COLS, 128), bf),
            pltpu.VMEM((2, 256, 128), bf), pltpu.VMEM((2, 256, 128), bf),
            pltpu.VMEM((4, 2, 256, 128), f32), pltpu.VMEM((2, 272, 128), f32),
            pltpu.VMEM((PIECES, 4, 2, COLS, 128), bf), pltpu.VMEM((2, 4, 4, 2, COLS, 128), bf),
            pltpu.VMEM((4, 2, COLS, 128), bf), pltpu.VMEM((4, 2, COLS, 128), bf),
            pltpu.VMEM((PIECES, 3, 2, COLS, 128), bf),
            dma((2, PIECES)), dma((2, PIECES)), dma((2,)), dma((2,)), dma((PIECES,)), dma((2, 4)),
            dma, dma, dma((PIECES,)), dma((PIECES,)),
        ],
        compiler_params=pltpu.CompilerParams(collective_id=0, has_side_effects=True, vmem_limit_bytes=40 << 20),
    )(friction, dep, flags)


def per_device(particle_mass, particle_velocity, spline_weights, particle_cells, block_counts, friction, contact_flags):
    dep = deposit((8, 2, 0), block_counts.reshape(32), particle_mass, particle_velocity, spline_weights, particle_cells)
    return exchange(friction, dep, contact_flags)


def solution(mesh):
    return jax.shard_map(
        per_device,
        mesh=mesh,
        in_specs=(
            P("mat", "gz"),
            P("mat", None, "gz"),
            P("mat", None, "gz"),
            P("mat", "gz"),
            P("mat", "gz", None),
            P("mat"),
            P("gz", None, None),
        ),
        out_specs=P("mat", None, "gz", None, None),
        check_vma=False,
    )
```
